128 devices in a mesh: dp: 64 (over y, x_hi, z, core), tensor: 2 (over x_lo).
Axes of the slice: x: 4 (x_hi: 2, x_lo: 2; x = x_hi * 2 + x_lo), y: 4, z: 4, core: 2. Of those that a mesh axis runs over, the one named last changes fastest.
Arguments:
- layer_input: bfloat16 [32768, 768], P(('dp', 'tensor')), may hold values from -24 to 24
- segment_starts: int32 [32768], P('dp'), may hold values from 0 to 511, as said below
- norm_gains: bfloat16 [2, 768], P(None, 'dp'), may hold values from 0.5 to 1.5
- norm_shifts: bfloat16 [2, 768], P(None, 'dp'), may hold values from -3 to 3
- projection: bfloat16 [768, 3, 768], P('dp', None, 'tensor'), may hold values from -0.3125 to 0.3125
- triple_bias: bfloat16 [3, 768], P(None, ('tensor', 'dp')), may hold values from -3 to 3
- dense_weight: bfloat16 [768, 768], P('tensor', 'dp'), may hold values from -0.625 to 0.625
- inner_weight: bfloat16 [768, 3072], P('dp', 'tensor'), may hold values from -0.21875 to 0.21875
- unit_bias: bfloat16 [3072], P(('tensor', 'dp')), may hold values from -3 to 3
- outer_weight: bfloat16 [3072, 768], P('tensor', 'dp'), may hold values from -0.15625 to 0.15625
- final_bias: bfloat16 [768], P('dp'), may hold values from -3 to 3
- cotangent: bfloat16 [32768, 768], P(('dp', 'tensor')), may hold values from -24 to 24
Outputs:
- layer_output: bfloat16 [32768, 768], P(('dp', 'tensor'))
- input_grad: bfloat16 [32768, 768], P(('dp', 'tensor'))
- gains_grad: float32 [2, 768], P(None, ('dp', 'tensor'))
- shifts_grad: float32 [2, 768], P(None, ('dp', 'tensor'))
- projection_grad: float32 [768, 3, 768], P('dp', None, 'tensor')
- triple_grad: float32 [3, 768], P(None, ('tensor', 'dp'))
- dense_grad: float32 [768, 768], P('tensor', 'dp')
- inner_grad: float32 [768, 3072], P('dp', 'tensor')
- units_grad: float32 [3072], P(('tensor', 'dp'))
- outer_grad: float32 [3072, 768], P('tensor', 'dp')
- final_grad: float32 [768], P(('dp', 'tensor'))
The draws below stay inside these ranges and needn't reach their ends.
Inputs may be any that keep to these rules, and one draw needn't show every extreme that they name: `segment_starts`: each token's entry is the index, within its group of 512 consecutive tokens, of the first token of its sequence; sequences never cross groups and hold at most 512 tokens, and some sequence holds exactly 512.
All inputs are finite; a program needn't handle non-finite values.
Results may differ from the reference program's by a relative error of at most 0.011.
Values may be sent and summed in bfloat16 or wider, within the bound.
A program may use at most 128 MiB of HBM per device.

```python
import math
import jax
import jax.numpy as jnp
from jax import lax

D = 768
HD = 64
FF = 3072
ROT = 16
GROUP = 512
SEQ_MOST = 512
TOKENS = 32768
N_DP = 64


def draw_segment_starts(key, part):
    key = jax.random.fold_in(key, 11)
    first_key, second_key, third_key = jax.random.split(key, 3)
    rates = jax.random.randint(first_key, (N_DP, 1), 2, 65)
    marks = jax.random.randint(second_key, (N_DP, GROUP), 0, 1 << 20) % rates == 0
    chosen = jax.random.randint(third_key, (), 0, N_DP)
    places = jnp.arange(GROUP, dtype=jnp.int32)
    forced = places % SEQ_MOST == (GROUP // 2 + SEQ_MOST // 2) % SEQ_MOST
    owners = jnp.arange(N_DP, dtype=jnp.int32)[:, None]
    marks = marks & (places[None, :] != GROUP // 2) & (owners != chosen)
    begins = marks | forced[None, :] | (places[None, :] == 0)
    starts = lax.cummax(jnp.where(begins, places[None, :], 0), axis=1)
    return starts.reshape(N_DP * GROUP).astype(jnp.int32)


def spiked(drawn, key, source, target, parts, factor):
    owner, partner = [(jnp.arange(drawn.shape[axis_at]) // (drawn.shape[axis_at] // parts)).reshape([-1 if axis == axis_at else 1 for axis in range(drawn.ndim)]) for axis_at in (source, target)]
    chosen = jax.random.permutation(key, parts)[partner]
    strong = (owner == chosen) | (owner == (partner + parts // 2) % parts)
    return jnp.where(strong, factor * drawn, drawn)


def steps_of(rng, dims, cuts, least, high):
    gain = 1.0
    for axis_at, parts in cuts:
        steps = jax.random.uniform(jax.random.fold_in(jax.random.fold_in(rng, 6), axis_at), (parts,), jnp.float32, least / len(cuts), high / len(cuts))
        gain = gain * jnp.repeat(jnp.exp(steps), dims[axis_at] // parts).reshape((-1,) + (1,) * (len(dims) - 1 - axis_at))
    return gain


def scatter_about(stream_key, dims, scale, most, shards=(), held_as=jnp.bfloat16):
    entries = scale * jax.random.normal(stream_key, dims, jnp.float32)
    if shards:
        entries = entries * steps_of(stream_key, dims, shards, -0.22, 0.18)
    return jnp.clip(entries, -most, most).astype(held_as)


def bell_draw_with(rng, shape, deviation, bound, pieces, heavy, kind=jnp.bfloat16):
    result = deviation * jax.random.normal(rng, shape, jnp.float32)
    if pieces:
        result = result * steps_of(rng, shape, pieces, -0.22, 0.18)
    return jnp.clip(spiked(result, jax.random.fold_in(rng, 3), *heavy), -bound, bound).astype(kind)


def setup_inputs(seed: int = 0) -> dict:
    key_of = jax.random.split(jax.random.key(seed), 13)
    return {
        "layer_input": bell_draw_with(key_of[0], (TOKENS, D), 1.0, 24.0, ((0, 128),), (0, 1, 128, 5.5)),
        "segment_starts": draw_segment_starts(jax.random.fold_in(key_of[12], 71), 0),
        "norm_gains": jnp.clip(1.0 + 0.1 * jax.random.normal(key_of[2], (2, D), jnp.float32), 0.5, 1.5).astype(jnp.bfloat16),
        "norm_shifts": scatter_about(key_of[3], (2, D), 0.3, 3.0, ((1, 64),)),
        "projection": scatter_about(key_of[4], (D, 3, D), (D // 2) ** -0.5, 0.3125, ((0, 64), (2, 2))),
        "triple_bias": scatter_about(key_of[5], (3, D), 0.3, 3.0, ((1, 128),)),
        "dense_weight": scatter_about(key_of[6], (D, D), (D // 8) ** -0.5, 0.625, ((0, 2), (1, 64))),
        "inner_weight": scatter_about(key_of[7], (D, FF), D ** -0.5, 0.21875, ((0, 64), (1, 2))),
        "unit_bias": scatter_about(key_of[8], (FF,), 0.3, 3.0, ((0, 128),)),
        "outer_weight": scatter_about(key_of[9], (FF, D), (FF // 2) ** -0.5, 0.15625, ((0, 2), (1, 64))),
        "final_bias": scatter_about(key_of[10], (D,), 0.3, 3.0, ((0, 64),)),
        "cotangent": bell_draw_with(key_of[11], (TOKENS, D), 1.0, 24.0, ((0, 128),), (0, 1, 128, 5.5)),
    }


EPSILON = 1e-05
BLOCK_ROWS = 512
HIGHEST = lax.Precision.HIGHEST

@jax.custom_vjp
def low(v):
    return lax.optimization_barrier(v.astype(jnp.bfloat16)).astype(jnp.float32)

@jax.custom_vjp
def low_back(v):
    return v

def low_keep(v):
    return (low(v), None)

def low_pass(kept, grad):
    return (grad,)

def back_keep(v):
    return (v, None)

def back_low(kept, grad):
    return (low(grad),)
low.defvjp(low_keep, low_pass)
low_back.defvjp(back_keep, back_low)

def normalize(field):
    center = lax.optimization_barrier(jnp.mean(field, axis=-1, keepdims=True))
    centred = field - center
    spread = lax.optimization_barrier(jnp.mean(centred * centred, axis=-1, keepdims=True))
    return centred * lax.rsqrt(spread + EPSILON)

def angles_for(starts):
    group_size = starts.shape[0]
    places = (jnp.arange(group_size, dtype=jnp.int32) - starts).astype(jnp.float32)
    freqs = jnp.exp(jnp.arange(ROT // 2, dtype=jnp.float32) * (-2.0 * math.log(10000.0) / ROT))
    turns = places[:, None] * freqs[None, :]
    return (jnp.cos(turns)[:, None, :], jnp.sin(turns)[:, None, :])

def rotate(field, cosine_table, sine_table):
    half_rot = ROT // 2
    first = field[..., :half_rot]
    second = field[..., half_rot:ROT]
    return jnp.concatenate([first * cosine_table - second * sine_table, second * cosine_table + first * sine_table, field[..., ROT:]], axis=-1)

def attention(queries, key_rows, values, starts):
    group_size = queries.shape[0]
    block_rows = min(BLOCK_ROWS, group_size)
    places = jnp.arange(group_size, dtype=jnp.int32)
    score_scale = 1.0 / math.sqrt(HD)

    def attend(block_index):
        row_begin = (block_index * block_rows).astype(jnp.int32)
        query_block = lax.dynamic_slice_in_dim(queries, row_begin, block_rows)
        row_places = lax.dynamic_slice_in_dim(places, row_begin, block_rows)
        row_starts = lax.dynamic_slice_in_dim(starts, row_begin, block_rows)
        allowed = (row_starts[:, None] == starts[None, :]) & (places[None, :] <= row_places[:, None])
        raw_scores = low_back(jnp.einsum('qhd,khd->hqk', query_block, key_rows, precision=HIGHEST) * score_scale)
        scores = jnp.where(allowed[None], raw_scores, -1e+30)
        row_peak = lax.optimization_barrier(jnp.max(scores, axis=-1, keepdims=True))
        powers = jnp.exp(scores - row_peak)
        probs = low(powers / lax.optimization_barrier(jnp.sum(powers, axis=-1, keepdims=True)))
        return jnp.einsum('hqk,khd->qhd', probs, values, precision=HIGHEST)
    blocks = lax.map(jax.checkpoint(attend), jnp.arange(group_size // block_rows, dtype=jnp.int32))
    return blocks.reshape(group_size, D)

def layer(field, starts, norm_gains, norm_shifts, projection, triple_bias, dense_weight, inner_weight, unit_bias, outer_weight, final_bias):
    group_size = field.shape[0]
    heads = D // HD
    normal_rows = normalize(field)
    first_in = low(normal_rows * norm_gains[0] + norm_shifts[0])
    second_in = low(normal_rows * norm_gains[1] + norm_shifts[1])
    cosine_table, sine_table = angles_for(starts)
    triple = jnp.einsum('td,dke->kte', first_in, projection, precision=HIGHEST) + triple_bias[:, None, :]
    queries = low(rotate(low_back(triple[0]).reshape(group_size, heads, HD), cosine_table, sine_table))
    key_rows = low(rotate(low_back(triple[1]).reshape(group_size, heads, HD), cosine_table, sine_table))
    values = low(low_back(triple[2])).reshape(group_size, heads, HD)
    context = low_back(low(attention(queries, key_rows, values, starts)))
    attend_part = jnp.dot(context, dense_weight, precision=HIGHEST)
    inner_pre = low_back(jnp.dot(second_in, inner_weight, precision=HIGHEST) + unit_bias)
    active = low(jax.nn.gelu(inner_pre, approximate=False))
    feed_part = jnp.dot(active, outer_weight, precision=HIGHEST)
    return field + attend_part + feed_part + final_bias

def reference(layer_input, segment_starts, norm_gains, norm_shifts, projection, triple_bias, dense_weight, inner_weight, unit_bias, outer_weight, final_bias, cotangent):
    params = tuple((item.astype(jnp.float32) for item in (norm_gains, norm_shifts, projection, triple_bias, dense_weight, inner_weight, unit_bias, outer_weight, final_bias)))
    inputs = layer_input.astype(jnp.float32).reshape(N_DP, GROUP, D)
    upstream = cotangent.astype(jnp.float32).reshape(N_DP, GROUP, D)
    starts = segment_starts.reshape(N_DP, GROUP)

    def visit(carried, item):
        field, group_starts, group_upstream = item

        def forward(residual, *weights):
            return layer(residual, group_starts, *weights)
        output, pullback = jax.vjp(forward, field, *params)
        grads = pullback(group_upstream)
        summed = tuple((left + right for left, right in zip(carried, grads[1:])))
        return (summed, (output, grads[0]))
    initial = tuple((jnp.zeros_like(item) for item in params))
    totals, (outputs, input_grads) = lax.scan(visit, initial, (inputs, starts, upstream))
    layer_output = outputs.reshape(TOKENS, D).astype(jnp.bfloat16)
    input_grad = input_grads.reshape(TOKENS, D).astype(jnp.bfloat16)
    return (layer_output, input_grad, totals[0], totals[1], totals[2], totals[3], totals[4], totals[5], totals[6], totals[7], totals[8])
```

```python
import math

import jax
import jax.numpy as jnp
import numpy as np
from jax import lax
from jax.experimental import pallas as pl
from jax.experimental.pallas import tpu as pltpu
from jax.sharding import PartitionSpec as P

MESH = pl.DeviceIdType.MESH
F32, BF16 = jnp.float32, jnp.bfloat16

D, HD, ROT = 768, 64, 16
T, HALF_T = 512, 256
EPSILON = 1e-05
Y, XH, Z, CORE = 4, 2, 4, 2
OWN = 12
PAD = 16
BLK = OWN * XH * CORE
PROJ, SMALL, DENSE, INNER, OUTER, COLS = 0, 1152, 1280, 1664, 3200, 4864
HALF = COLS // 2
PART = ((0, 1280), (1280, 1152))
CUT = ((0, 640, 640), (0, 640, 512))
VEC = 5 * D + 3 * 384 + 1536
OFF_TB, OFF_UB = 5 * OWN, 5 * OWN + 18
VMEM_LIMIT = 56 * 1024 * 1024


def order_tables():
    j = np.arange(64)
    c, xh, z, y = j % 2, (j // 2) % 2, (j // 4) % 4, j // 16
    dp = ((y * 2 + xh) * 4 + z) * 2 + c
    at = (12 * dp[:, None] + np.arange(12)[None, :]).reshape(-1)
    perm = np.zeros((D, D), np.float32)
    perm[at, np.arange(D)] = 1
    spread = np.zeros((128, VEC), np.float32)
    mask = np.zeros((64, VEC), np.float32)
    col = np.arange(D)
    for v in range(5):
        spread[v * 12 + col % 12, v * D + col] = 1
        mask[col // 12, v * D + col] = 1
    back = np.argsort(dp)
    col = np.arange(384)
    for k in range(3):
        spread[OFF_TB + 6 * k + col % 6, 5 * D + 384 * k + col] = 1
        mask[back[col // 6], 5 * D + 384 * k + col] = 1
    col = np.arange(1536)
    spread[OFF_UB + col % 24, 5 * D + 1152 + col] = 1
    mask[back[col // 24], 5 * D + 1152 + col] = 1
    rows = np.zeros((D, 64), np.float32)
    rows[12 * j, j] = 1
    pick = np.zeros((BLK, 64), np.float32)
    r = np.arange(BLK)
    pick[r, 16 * (r // 12) + r % 12] = 1
    return [m.astype(jnp.bfloat16) for m in (perm, spread, mask, rows, np.ascontiguousarray(rows.T), pick, np.ascontiguousarray(pick.T))]


def nn(a, b):
    return lax.dot_general(a, b, (((1,), (0,)), ((), ())), preferred_element_type=F32)


def nt(a, b):
    return lax.dot_general(a, b, (((1,), (1,)), ((), ())), preferred_element_type=F32)


def tn(a, b):
    return lax.dot_general(a, b, (((0,), (0,)), ((), ())), preferred_element_type=F32)


class Place:
    def __init__(self):
        dp = lax.axis_index("dp")
        self.t = lax.axis_index("tensor")
        self.c = lax.rem(dp, 2)
        self.z = lax.rem(lax.div(dp, 2), 4)
        self.xh = lax.rem(lax.div(dp, 8), 2)
        self.y = lax.div(dp, 16)
        self.slot = self.xh * 2 + self.c

    def dev(self, y=None, xh=None, z=None, c=None, t=None):
        y = self.y if y is None else y
        xh = self.xh if xh is None else xh
        z = self.z if z is None else z
        c = self.c if c is None else c
        t = self.t if t is None else t
        return (((y * 2 + xh) * 4 + z) * 2 + c, t)

    def ring(self, axis, step):
        at = lax.rem((self.y if axis == "y" else self.z) + step, 4)
        return self.dev(y=at) if axis == "y" else self.dev(z=at)

    def quad(self, r):
        c = 1 - self.c if r & 1 else self.c
        xh = 1 - self.xh if r & 2 else self.xh
        return self.dev(xh=xh, c=c), xh, c

    def peers(self):
        out = [self.quad(r)[0] for r in (1, 2, 3)]
        for axis in ("y", "z"):
            out += [self.ring(axis, 1), self.ring(axis, 3)]
        return out + [self.dev(t=1 - self.t)]


def enter(place):
    barrier = pltpu.get_barrier_semaphore()
    peers = place.peers()
    for peer in peers:
        pl.semaphore_signal(barrier, inc=1, device_id=peer, device_id_type=MESH)
    pl.semaphore_wait(barrier, len(peers))


def remote(src, dst, send, recv, device):
    copy = pltpu.make_async_remote_copy(
        src_ref=src, dst_ref=dst, send_sem=send, recv_sem=recv, device_id=device, device_id_type=MESH
    )
    copy.start()
    return copy


AXES = (("y", "z"), ("z", "y"))


def cols_of(core, part, piece=None):
    begin, width = PART[part]
    if piece is not None:
        first, second = CUT[part][1:]
        begin, width = (begin, first) if piece == 0 else (begin + first, second)
    return pl.ds(pl.multiple_of(core * HALF + begin, 128), width)


def gather_kernel(
    mine, x, cot, pick, w, xall, cotall, quad, blk, qsend, qrecv, rsend, rrecv, ssend, srecv, tsend, trecv, lsem
):
    me = Place()
    enter(me)
    partner = me.dev(t=1 - me.t)
    rows = pl.ds(pl.multiple_of(me.t * HALF_T, HALF_T), HALF_T)
    waits = []
    quads = []
    for r in (1, 2, 3):
        device, _, c = me.quad(r)
        quads.append(
            remote(
                mine.at[:, pl.ds(pl.multiple_of(c * HALF, 128), HALF)],
                quad.at[me.slot],
                qsend.at[r],
                qrecv.at[r],
                device,
            )
        )
    for i, (src, dst) in enumerate(((x, xall), (cot, cotall))):
        waits.append(remote(src, dst.at[rows], tsend.at[i], trecv.at[i], partner))
        local = pltpu.make_async_copy(src, dst.at[rows], lsem.at[i])
        local.start()
        waits.append(local)
    quad[me.slot] = mine[:, pl.ds(pl.multiple_of(me.c * HALF, 128), HALF)]
    for copy in quads:
        copy.wait_recv()
    blk[...] = nn(pick[...], quad[...].reshape(64, HALF)).astype(BF16)

    sibling = me.dev(c=1 - me.c)
    half = pl.ds(pl.multiple_of(me.c * HALF, 128), HALF)
    keep = pltpu.make_async_copy(blk, w.at[me.y, me.z, :, half], lsem.at[2])
    keep.start()
    waits.append(remote(blk, w.at[me.y, me.z, :, half], ssend.at[0], srecv.at[0], sibling))

    def share(index, ref):
        waits.append(remote(ref, ref, ssend.at[index], srecv.at[index], sibling))

    def unit(part, phase, step, piece=None):
        cols = cols_of(me.c, part, piece)
        axis = AXES[part][phase]
        y, z = me.y, me.z
        if axis == "y":
            y = lax.rem(y + step, 4)
        else:
            z = lax.rem(z + step, 4)
        if phase == 0:
            return w.at[y, z, :, cols]
        return w.at[y, :, :, cols] if axis == "y" else w.at[:, z, :, cols]

    for phase in range(2):
        copies = {}
        for part in range(2):
            axis = AXES[part][phase]
            for i, step in enumerate((1, 3)):
                src = unit(part, phase, 0)
                if phase == 0:
                    src = blk.at[:, pl.ds(*PART[part])]
                copies[part, i] = remote(
                    src,
                    unit(part, phase, 0),
                    rsend.at[part, phase, i],
                    rrecv.at[part, phase, i],
                    me.ring(axis, step),
                )
        for part in range(2):
            axis = AXES[part][phase]
            for i, step in enumerate((1, 3)):
                copies[part, i].wait_recv()
                ref = unit(part, phase, 4 - step, i)
                copies[part, 2 + i] = remote(
                    ref, ref, rsend.at[part, phase, 2 + i], rrecv.at[part, phase, 2 + i], me.ring(axis, step)
                )
        for part in range(2):
            for i, step in enumerate((1, 3)):
                share(1 + part * 6 + phase * 3 + i, unit(part, phase, 4 - step))
        for part in range(2):
            for i in range(2):
                copies[part, 2 + i].wait_recv()
            share(1 + part * 6 + phase * 3 + 2, unit(part, phase, 2))
        if phase == 0:
            keep.wait()
        for copy in copies.values():
            copy.wait_send()
    for copy in quads:
        copy.wait_send()
    for copy in waits:
        copy.wait()


def compute_kernel(
    w, x, cot, perm, spread, mask, rows_at, rows_of, cos_t, left_t, right_t, start_col, start_row,
    g, base_out, out_send, nb_own, nb_send, hat_own, fac_own, up_own,
    s1, s2, up, s1t, s2t, upt, hat, fac, q, k, v, cb, ctx, tb, act, ub, outp, nbp, vec, gvec,
):
    gvec[...] = jnp.zeros_like(gvec)
    small = nn(rows_of[...], w[:, SMALL:DENSE]).astype(BF16)
    for begin in range(0, VEC, D):
        width = min(D, VEC - begin)
        cols = slice(begin, begin + width)
        picked = nn(small, spread[:, cols]) * mask[:, cols].astype(F32)
        vec[:, cols] = jnp.broadcast_to(jnp.sum(picked, axis=0, keepdims=True), (8, width))

    def rowvec(begin, width):
        return vec[0:1, pl.ds(begin, width)]

    g0, g1, h0, h1, fb = (vec[0:1, i * D : (i + 1) * D] for i in range(5))

    def norm_rows(i, carry):
        rows = pl.ds(pl.multiple_of(i * 128, 128), 128)
        field = nn(x[rows, :], perm[...])
        center = jnp.mean(field, axis=-1, keepdims=True)
        centred = field - center
        factor = lax.rsqrt(jnp.mean(centred * centred, axis=-1, keepdims=True) + EPSILON)
        normal = centred * factor
        hat[rows, :] = normal
        fac[rows, :] = jnp.broadcast_to(factor, (128, 128))
        first = normal * g0 + h0
        second = normal * g1 + h1
        upstream = nn(cot[rows, :], perm[...])
        s1[rows, :] = first.astype(BF16)
        s2[rows, :] = second.astype(BF16)
        up[rows, :] = upstream.astype(BF16)
        outp[rows, :] = field + fb
        s1t[:, rows] = first.astype(BF16).T
        s2t[:, rows] = second.astype(BF16).T
        upt[:, rows] = upstream.astype(BF16).T
        gvec[0:1, 4 * D : 5 * D] += jnp.sum(upstream, axis=0, keepdims=True)
        return carry

    lax.fori_loop(0, 4, norm_rows, 0)

    def rotated(field, cosine, left, right, sign):
        n = field.shape[1]
        reps = n // 128
        wide = lambda table: jnp.concatenate([table] * reps, axis=1) if reps > 1 else table
        turned = pltpu.roll(field, n - 8, 1) * wide(left) + pltpu.roll(field, 8, 1) * wide(right)
        return field * wide(cosine) + sign * turned

    def heads_in(i, carry):
        cols = pl.ds(pl.multiple_of(i * 128, 128), 128)
        for n, ref in enumerate((q, k, v)):
            at = pl.ds(pl.multiple_of(PROJ + n * 384 + i * 128, 128), 128)
            field = nn(s1[...], w[:, at]) + rowvec(pl.multiple_of(5 * D + n * 384 + i * 128, 128), 128)
            if n < 2:
                field = rotated(field, cos_t[...], left_t[...], right_t[...], 1.0)
            ref[:, cols] = field.astype(BF16)
        cb[:, cols] = nn(up[...], w[:, pl.ds(pl.multiple_of(DENSE + i * 128, 128), 128)]).astype(BF16)
        return carry

    lax.fori_loop(0, 3, heads_in, 0)

    scale = 1.0 / math.sqrt(HD)

    def attend(pair, carry):
        cols = pl.ds(pl.multiple_of(pair * 128, 128), 128)
        halves = []
        for head in range(2):
            inside = (lax.broadcasted_iota(jnp.int32, (1, 128), 1) // HD) == head
            grads_k, grads_v, outs, grads_q = [], [], [], []
            for block in range(2):
                begin, n = block * HALF_T, (block + 1) * HALF_T
                rows = slice(begin, begin + HALF_T)
                kk, vv = k[0:n, cols], v[0:n, cols]
                qq = jnp.where(inside, q[rows, cols], 0).astype(BF16)
                cc = jnp.where(inside, cb[rows, cols], 0).astype(BF16)
                place_t = begin + lax.broadcasted_iota(jnp.int32, (HALF_T, n), 0)
                place_s = lax.broadcasted_iota(jnp.int32, (HALF_T, n), 1)
                allowed = (start_col[rows, 0:1] == start_row[0:1, 0:n]) & (place_s <= place_t)
                scores = jnp.where(allowed, nt(qq, kk) * scale, -1e30)
                powers = jnp.exp(scores - jnp.max(scores, axis=-1, keepdims=True))
                probs = powers / jnp.sum(powers, axis=-1, keepdims=True)
                low = probs.astype(BF16)
                outs.append(nn(low, vv))
                back = nt(cc, vv)
                inner = jnp.sum(probs * back, axis=-1, keepdims=True)
                ds = (probs * (back - inner)).astype(BF16)
                grads_q.append(nn(ds, kk) * scale)
                grads_k.append(tn(ds, qq) * scale)
                grads_v.append(tn(low, cc))
            join = lambda parts: jnp.concatenate([parts[1][:HALF_T] + parts[0], parts[1][HALF_T:]], axis=0)
            halves.append(
                (jnp.concatenate(outs, axis=0), jnp.concatenate(grads_q, axis=0), join(grads_k), join(grads_v))
            )
        first = (lax.broadcasted_iota(jnp.int32, (1, 128), 1) // HD) == 0
        out, dq, dk, dv = (jnp.where(first, a, b) for a, b in zip(*halves))
        ctx[:, cols] = out.astype(BF16)
        for n, field in enumerate((dq, dk, dv)):
            if n < 2:
                field = rotated(field, cos_t[...], left_t[...], right_t[...], -1.0)
            field = field.astype(BF16)
            tb[:, pl.ds(pl.multiple_of(n * 384 + pair * 128, 128), 128)] = field
            gvec[0:1, pl.ds(pl.multiple_of(5 * D + n * 384 + pair * 128, 128), 128)] = jnp.sum(
                field.astype(F32), axis=0, keepdims=True
            )
        return carry

    lax.fori_loop(0, 3, attend, 0)

    def units(i, carry):
        def at(begin):
            return pl.ds(pl.multiple_of(begin + i * 256, 128), 256)

        pre = nn(s2[...], w[:, at(INNER)]) + rowvec(pl.multiple_of(5 * D + 1152 + i * 256, 128), 256)
        phi = 0.5 * (1.0 + lax.erf(pre * (1.0 / math.sqrt(2.0))))
        act[:, at(0)] = (pre * phi).astype(BF16)
        slope = phi + pre * jnp.exp(-0.5 * pre * pre) * (1.0 / math.sqrt(2.0 * math.pi))
        back = (nn(up[...], w[:, at(OUTER)]) * slope).astype(BF16)
        ub[:, at(0)] = back
        gvec[0:1, at(5 * D + 1152)] = jnp.sum(back.astype(F32), axis=0, keepdims=True)
        return carry

    lax.fori_loop(0, 6, units, 0)

    def width_rows(i, carry):
        rows = pl.ds(pl.multiple_of(i * 256, 256), 256)

        def lanes(begin):
            return pl.ds(pl.multiple_of(begin + i * 256, 256), 256)

        outp[:, rows] += nt(ctx[...], w[rows, DENSE:INNER]) + nt(act[...], w[rows, OUTER : OUTER + 1536])
        second = nt(ub[...], w[rows, INNER:OUTER])
        first = nt(tb[...], w[rows, PROJ:SMALL])
        nbp[:, rows] = first * vec[0:1, lanes(0)] + second * vec[0:1, lanes(D)]
        normal = hat[:, rows]
        for n, term in enumerate((first * normal, second * normal, first, second)):
            gvec[0:1, lanes(n * D)] = jnp.sum(term, axis=0, keepdims=True)
        g[rows, PROJ:SMALL] = nn(s1t[rows, :], tb[...]).astype(BF16)
        g[rows, DENSE:INNER] = nn(upt[rows, :], ctx[...]).astype(BF16)
        g[rows, INNER:OUTER] = nn(s2t[rows, :], ub[...]).astype(BF16)
        g[rows, OUTER : OUTER + 1536] = nn(upt[rows, :], act[...]).astype(BF16)
        g[rows, OUTER + 1536 : COLS] = jnp.zeros((256, COLS - OUTER - 1536), BF16)
        return carry

    lax.fori_loop(0, 3, width_rows, 0)

    tile = jnp.zeros((64, 128), F32)
    for begin in range(0, VEC, D):
        width = min(D, VEC - begin)
        cols = slice(begin, begin + width)
        tile += nt((gvec[0:1, cols] * mask[:, cols].astype(F32)).astype(BF16), spread[:, cols])
    g[:, SMALL:DENSE] = nn(rows_at[...], tile.astype(BF16)).astype(BF16)

    side = lax.axis_index("tensor")
    own = pl.ds(pl.multiple_of(side * HALF_T, HALF_T), HALF_T)
    other = pl.ds(pl.multiple_of((1 - side) * HALF_T, HALF_T), HALF_T)
    residual = nn(x[other, :], perm[...]) + fb
    out_send[...] = (outp[other, :] - residual).astype(BF16)
    base_out[...] = outp[own, :]
    nb_send[...] = nbp[other, :].astype(BF16)
    nb_own[...] = nbp[own, :]
    hat_own[...] = hat[own, :]
    fac_own[...] = fac[own, :]
    up_own[...] = up[own, :]


def reduce_kernel(
    g, base_out, out_send, nb_own, nb_send, hat_own, fac_own, up_own, perm, pick_t,
    out, grad, small_out, rows_out,
    total, land, a1, a2, a3, a4, b1, b2, b3, b4, red, quad_send, quad_land, out_land, nb_land, small_land, small_mine,
    psend, precv, lsem, csend, crecv, rsend, rrecv, qsend, qrecv, esend, erecv,
):
    me = Place()
    enter(me)
    partner = me.dev(t=1 - me.t)
    sibling = me.dev(c=1 - me.c)
    waits = [
        remote(out_send, out_land, psend.at[0], precv.at[0], partner),
        remote(nb_send, nb_land, psend.at[1], precv.at[1], partner),
    ]
    axes = (("z", "y"), ("y", "z"))

    def block(ref, part, step, piece=None, core=None):
        begin, width = PART[part]
        if piece is not None:
            first, second = CUT[part][1:]
            begin, width = (begin, first) if piece == 0 else (begin + first, second)
        if core is not None:
            cols = pl.ds(pl.multiple_of(core * HALF + begin, 128), width)
        else:
            cols = pl.ds(begin, width)
        if axes[part][0] == "y":
            return ref.at[lax.rem(me.y + step, 4), :, :, cols]
        return ref.at[:, lax.rem(me.z + step, 4), :, cols]

    order = [(step, part) for step in (2, 1, 3, 0) for part in range(2)]
    pulls = {}
    for n, (step, part) in enumerate(order):
        local = pltpu.make_async_copy(block(g, part, step, core=me.c), block(total, part, step), lsem.at[n])
        local.start()
        copy = remote(
            block(g, part, step, core=1 - me.c), block(land, part, step), csend.at[n], crecv.at[n], sibling
        )
        pulls[step, part] = (local, copy)

    def add(dst, *terms):
        def body(i, carry):
            sum_ = dst[i].astype(F32)
            for term in terms:
                sum_ += term[i].astype(F32)
            dst[i] = sum_.astype(BF16)
            return carry

        lax.fori_loop(0, 4, body, 0)

    def join(step, part):
        local, copy = pulls[step, part]
        local.wait()
        copy.wait_recv()
        add(block(total, part, step), block(land, part, step))

    land1 = ((a1, a2, a3, a4), (b1, b2, b3, b4))
    copies = {}
    for part in range(2):
        join(2, part)
        for i, step in enumerate((1, 3)):
            copies[part, i] = remote(
                block(total, part, 2, i), land1[part][i], rsend.at[part, 0, i], rrecv.at[part, 0, i],
                me.ring(axes[part][0], step),
            )
    for part in range(2):
        for i, step in enumerate((1, 3)):
            join(step, part)
            copies[part, i].wait_recv()
            add(block(total, part, step, i), land1[part][i])
            copies[part, 2 + i] = remote(
                block(total, part, step), land1[part][2 + i], rsend.at[part, 0, 2 + i], rrecv.at[part, 0, 2 + i],
                me.ring(axes[part][0], step),
            )
    for part in range(2):
        join(0, part)
    for copy in waits:
        copy.wait()

    def finish(i, carry):
        rows = pl.ds(pl.multiple_of(i * 64, 64), 64)
        low = (base_out[rows, :] + out_land[rows, :].astype(F32)).astype(BF16)
        out[rows, :] = nt(low, perm[...]).astype(BF16)
        back = nb_own[rows, :] + nb_land[rows, :].astype(F32)
        normal = hat_own[rows, :]
        value = up_own[rows, :].astype(F32) + fac_own[rows, 0:1] * (
            back
            - jnp.mean(back, axis=-1, keepdims=True)
            - normal * jnp.mean(back * normal, axis=-1, keepdims=True)
        )
        grad[rows, :] = nt(value.astype(BF16), perm[...]).astype(BF16)
        return carry

    lax.fori_loop(0, 4, finish, 0)

    for part in range(2):
        for i in range(2):
            copies[part, 2 + i].wait_recv()
        add(block(total, part, 0), land1[part][2], land1[part][3])
    for copy in copies.values():
        copy.wait_send()

    def piece_of(part, step, piece=None):
        begin, width = PART[part]
        if piece is not None:
            first, second = CUT[part][1:]
            begin, width = (begin, first) if piece == 0 else (begin + first, second)
        cols = pl.ds(begin, width)
        if axes[part][1] == "y":
            return total.at[lax.rem(me.y + step, 4), me.z, :, cols]
        return total.at[me.y, lax.rem(me.z + step, 4), :, cols]

    land2 = []
    for part in range(2):
        begin, width = PART[part]
        first, second = CUT[part][1:]
        land2.append(
            (
                red.at[0, :, pl.ds(begin, first)],
                red.at[0, :, pl.ds(begin + first, second)],
                red.at[1, :, pl.ds(begin, width)],
                red.at[2, :, pl.ds(begin, width)],
            )
        )
    more = {}
    for part in range(2):
        for i, step in enumerate((1, 3)):
            more[part, i] = remote(
                piece_of(part, 2, i), land2[part][i], rsend.at[part, 1, i], rrecv.at[part, 1, i],
                me.ring(axes[part][1], step),
            )
    for part in range(2):
        for i, step in enumerate((1, 3)):
            more[part, i].wait_recv()
            piece = piece_of(part, step, i)
            piece[...] = (piece[...].astype(F32) + land2[part][i][...].astype(F32)).astype(BF16)
            more[part, 2 + i] = remote(
                piece_of(part, step), land2[part][2 + i], rsend.at[part, 1, 2 + i], rrecv.at[part, 1, 2 + i],
                me.ring(axes[part][1], step),
            )
    for part in range(2):
        begin, width = PART[part]
        for i in range(2):
            more[part, 2 + i].wait_recv()
        sum_ = (
            total[me.y, me.z, :, pl.ds(begin, width)].astype(F32)
            + land2[part][2][...].astype(F32)
            + land2[part][3][...].astype(F32)
        )
        quad_send[:, :, pl.ds(begin, width)] = (
            nn(pick_t[...], sum_.astype(BF16)).astype(BF16).reshape(4, PAD, width)
        )
    quads = []
    for r in (1, 2, 3):
        device, xh, c = me.quad(r)
        quads.append(remote(quad_send.at[xh * 2 + c], quad_land.at[me.slot], qsend.at[r], qrecv.at[r], device))
    quad_land[me.slot] = quad_send[me.slot]
    for copy in quads:
        copy.wait_recv()
    for c in range(2):
        rows_out[:, c * HALF : (c + 1) * HALF] = quad_land[c].astype(F32) + quad_land[2 + c].astype(F32)
    small_mine[...] = rows_out[:, SMALL:DENSE]
    last = remote(small_mine, small_land, esend, erecv, partner)
    for copy in more.values():
        copy.wait_send()
    for copy in quads:
        copy.wait_send()
    for local, copy in pulls.values():
        copy.wait_send()
    last.wait()
    lane = lax.broadcasted_iota(jnp.int32, (PAD, 128), 1)
    small_out[...] = small_mine[...] + jnp.where(lane < 4 * OWN, small_land[...], 0.0)


def turn_tables(starts):
    places = (jnp.arange(T, dtype=jnp.int32) - starts).astype(F32)
    lane = jnp.arange(128, dtype=jnp.int32) % HD
    freqs = jnp.exp((lane % 8).astype(F32) * (-2.0 * math.log(10000.0) / ROT))
    turns = places[:, None] * freqs[None, :]
    cosine, sine = jnp.cos(turns), jnp.sin(turns)
    return (
        jnp.where(lane < ROT, cosine, 1.0),
        jnp.where(lane < 8, -sine, 0.0),
        jnp.where((lane >= 8) & (lane < ROT), sine, 0.0),
    )


def local(
    layer_input, segment_starts, norm_gains, norm_shifts, projection, triple_bias, dense_weight, inner_weight,
    unit_bias, outer_weight, final_bias, cotangent,
):
    perm, spread, mask, rows_at, rows_of, pick, pick_t = [jnp.asarray(m) for m in order_tables()]
    small = jnp.concatenate(
        [norm_gains.reshape(-1), norm_shifts.reshape(-1), final_bias, triple_bias.reshape(-1), unit_bias]
    )
    small = jnp.pad(small[None, :], ((0, OWN - 1), (0, 128 - small.shape[0])))
    mine = jnp.concatenate(
        [
            projection.reshape(OWN, 1152),
            small,
            dense_weight.T,
            inner_weight,
            outer_weight.T,
            jnp.zeros((OWN, 128), BF16),
        ],
        axis=1,
    )
    mine = jnp.pad(mine, ((0, PAD - OWN), (0, 0)))
    vm = pl.BlockSpec(memory_space=pltpu.VMEM)
    anywhere = pl.BlockSpec(memory_space=pl.ANY)
    dma = pltpu.SemaphoreType.DMA
    struct = jax.ShapeDtypeStruct

    w, xall, cotall = pl.pallas_call(
        gather_kernel,
        out_shape=(struct((Y, Z, BLK, COLS), BF16), struct((T, D), BF16), struct((T, D), BF16)),
        in_specs=[vm, anywhere, anywhere, vm],
        out_specs=(anywhere,) * 3,
        scratch_shapes=[
            pltpu.VMEM((4, PAD, HALF), BF16),
            pltpu.VMEM((BLK, HALF), BF16),
            dma((4,)), dma((4,)), dma((2, 2, 4)), dma((2, 2, 4)), dma((13,)), dma((13,)), dma((2,)), dma((2,)), dma((3,)),
        ],
        compiler_params=pltpu.CompilerParams(collective_id=0, has_side_effects=True),
        name="gather",
    )(mine, layer_input, cotangent, pick)

    tables = turn_tables(segment_starts)
    start_col = jnp.broadcast_to(segment_starts[:, None], (T, 128))
    start_row = jnp.broadcast_to(segment_starts[None, :], (8, T))
    rows = lambda kind, n=D: struct((HALF_T, n), kind)
    vmem = pltpu.VMEM
    g, base_out, out_send, nb_own, nb_send, hat_own, fac_own, up_own = pl.pallas_call(
        compute_kernel,
        out_shape=(
            struct((D, COLS), BF16), rows(F32), rows(BF16), rows(F32), rows(BF16), rows(F32), rows(F32, 128), rows(BF16),
        ),
        in_specs=[vm] * 13,
        out_specs=(vm,) * 8,
        scratch_shapes=[vmem((T, D), BF16)] * 3
        + [vmem((D, T), BF16)] * 3
        + [vmem((T, D), F32), vmem((T, 128), F32)]
        + [vmem((T, 384), BF16)] * 5
        + [vmem((T, 1152), BF16), vmem((T, 1536), BF16), vmem((T, 1536), BF16), vmem((T, D), F32), vmem((T, D), F32)]
        + [vmem((8, VEC), F32)] * 2,
        compiler_params=pltpu.CompilerParams(vmem_limit_bytes=VMEM_LIMIT),
        name="layer",
    )(
        w.reshape(D, COLS), xall, cotall, perm, spread, mask, rows_at, rows_of, *tables, start_col, start_row
    )

    out, grad, small_grad, rows_grad = pl.pallas_call(
        reduce_kernel,
        out_shape=(rows(BF16), rows(BF16), struct((PAD, 128), F32), struct((PAD, COLS), F32)),
        in_specs=[anywhere] + [vm] * 9,
        out_specs=(vm,) * 4,
        scratch_shapes=[
            vmem((Y, Z, BLK, HALF), BF16), vmem((Y, Z, BLK, HALF), BF16),
            vmem((4, BLK, 640), BF16), vmem((4, BLK, 640), BF16), vmem((4, BLK, 1280), BF16), vmem((4, BLK, 1280), BF16),
            vmem((4, BLK, 640), BF16), vmem((4, BLK, 512), BF16), vmem((4, BLK, 1152), BF16), vmem((4, BLK, 1152), BF16),
            vmem((3, BLK, HALF), BF16), vmem((4, PAD, HALF), BF16), vmem((4, PAD, HALF), BF16),
            vmem((HALF_T, D), BF16), vmem((HALF_T, D), BF16), vmem((PAD, 128), F32), vmem((PAD, 128), F32),
            dma((2,)), dma((2,)), dma((8,)), dma((8,)), dma((8,)), dma((2, 2, 4)), dma((2, 2, 4)), dma((4,)), dma((4,)),
            dma, dma,
        ],
        compiler_params=pltpu.CompilerParams(collective_id=1, has_side_effects=True, vmem_limit_bytes=VMEM_LIMIT),
        name="reduce",
    )(
        g.reshape(Y, Z, BLK, COLS), base_out, out_send, nb_own, nb_send, hat_own, fac_own, up_own, perm, pick_t
    )

    vals = small_grad[0]
    side = lax.axis_index("tensor")

    def six(field):
        return lax.dynamic_slice_in_dim(field, side * 6, 6, axis=field.ndim - 1)

    own = rows_grad[:OWN]
    return (
        out,
        grad,
        six(vals[0:24].reshape(2, OWN)),
        six(vals[24:48].reshape(2, OWN)),
        own[:, PROJ:SMALL].reshape(OWN, 3, 384),
        vals[OFF_TB:OFF_UB].reshape(3, 6),
        own[:, DENSE:INNER].T,
        own[:, INNER:OUTER],
        vals[OFF_UB : OFF_UB + 24],
        own[:, OUTER : OUTER + 1536].T,
        six(vals[48:60]),
    )


def solution(mesh):
    placed = (
        P(("dp", "tensor"), None),
        P("dp"),
        P(None, "dp"),
        P(None, "dp"),
        P("dp", None, "tensor"),
        P(None, ("tensor", "dp")),
        P("tensor", "dp"),
        P("dp", "tensor"),
        P(("tensor", "dp")),
        P("tensor", "dp"),
        P("dp"),
        P(("dp", "tensor"), None),
    )
    return jax.shard_map(
        local,
        mesh=mesh,
        in_specs=placed,
        out_specs=(
            P(("dp", "tensor"), None),
            P(("dp", "tensor"), None),
            P(None, ("dp", "tensor")),
            P(None, ("dp", "tensor")),
            P("dp", None, "tensor"),
            P(None, ("tensor", "dp")),
            P("tensor", "dp"),
            P("dp", "tensor"),
            P(("tensor", "dp")),
            P("tensor", "dp"),
            P(("dp", "tensor")),
        ),
        check_vma=False,
    )
```

```python
import math

import jax
import jax.numpy as jnp
import numpy as np
from jax import lax
from jax.experimental import pallas as pl
from jax.experimental.pallas import tpu as pltpu
from jax.sharding import PartitionSpec as P

MESH = pl.DeviceIdType.MESH
F32, BF16 = jnp.float32, jnp.bfloat16

D, HD, ROT = 768, 64, 16
T, HALF_T = 512, 256
EPSILON = 1e-05
Y, XH, Z, CORE = 4, 2, 4, 2
OWN = 12
PAD = 16
BLK = OWN * XH * CORE
COLS, WIDE = 4864, 2432
W_SMALL, W_DENSE, W_UNITS = 1152, 1280, (1792, 3328)
G_DENSE, G_INNER, G_OUTER, G_SMALL = 1152, (1536, 3072), (2304, 3968), 3840
EVEN = ((0, 384), (384, 384))
UNEVEN = ((0, 512), (512, 384))
W_GROUPS = ((0, 896, UNEVEN, 0), (1792, 768, EVEN, 896), (3328, 768, EVEN, 1664))
G_GROUPS = ((0, 768, EVEN, 0), (1536, 768, EVEN, 768), (3072, 896, UNEVEN, 1536))
VEC = 5 * D + 3 * 384 + 1536
OFF_TB, OFF_UB = 5 * OWN, 5 * OWN + 18
VMEM_LIMIT = 56 * 1024 * 1024


def order_tables():
    j = np.arange(64)
    c, xh, z, y = j % 2, (j // 2) % 2, (j // 4) % 4, j // 16
    dp = ((y * 2 + xh) * 4 + z) * 2 + c
    at = (12 * dp[:, None] + np.arange(12)[None, :]).reshape(-1)
    perm = np.zeros((D, D), np.float32)
    perm[at, np.arange(D)] = 1
    spread = np.zeros((128, VEC), np.float32)
    mask = np.zeros((64, VEC), np.float32)
    col = np.arange(D)
    for v in range(5):
        spread[v * 12 + col % 12, v * D + col] = 1
        mask[col // 12, v * D + col] = 1
    back = np.argsort(dp)
    col = np.arange(384)
    for k in range(3):
        spread[OFF_TB + 6 * k + col % 6, 5 * D + 384 * k + col] = 1
        mask[back[col // 6], 5 * D + 384 * k + col] = 1
    col = np.arange(1536)
    spread[OFF_UB + col % 24, 5 * D + 1152 + col] = 1
    mask[back[col // 24], 5 * D + 1152 + col] = 1
    rows = np.zeros((D, 64), np.float32)
    rows[12 * j, j] = 1
    pick = np.zeros((BLK, 64), np.float32)
    r = np.arange(BLK)
    pick[r, 16 * (r // 12) + r % 12] = 1
    return [m.astype(jnp.bfloat16) for m in (perm, spread, mask, rows, np.ascontiguousarray(rows.T), pick, np.ascontiguousarray(pick.T))]


def nn(a, b):
    return lax.dot_general(a, b, (((1,), (0,)), ((), ())), preferred_element_type=F32)


def nt(a, b):
    return lax.dot_general(a, b, (((1,), (1,)), ((), ())), preferred_element_type=F32)


def tn(a, b):
    return lax.dot_general(a, b, (((0,), (0,)), ((), ())), preferred_element_type=F32)


class Place:
    def __init__(self):
        dp = lax.axis_index("dp")
        self.t = lax.axis_index("tensor")
        self.c = lax.rem(dp, 2)
        self.z = lax.rem(lax.div(dp, 2), 4)
        self.xh = lax.rem(lax.div(dp, 8), 2)
        self.y = lax.div(dp, 16)
        self.slot = self.xh * 2 + self.c

    def dev(self, y=None, xh=None, z=None, c=None, t=None):
        y = self.y if y is None else y
        xh = self.xh if xh is None else xh
        z = self.z if z is None else z
        c = self.c if c is None else c
        t = self.t if t is None else t
        return (((y * 2 + xh) * 4 + z) * 2 + c, t)

    def ring(self, axis, step):
        at = lax.rem((self.y if axis == "y" else self.z) + step, 4)
        return self.dev(y=at) if axis == "y" else self.dev(z=at)

    def quad(self, r):
        c = 1 - self.c if r & 1 else self.c
        xh = 1 - self.xh if r & 2 else self.xh
        return self.dev(xh=xh, c=c), xh, c

    def peers(self):
        out = [self.quad(r)[0] for r in (1, 2, 3)]
        for axis in ("y", "z"):
            out += [self.ring(axis, step) for step in (1, 2, 3)]
        return out + [self.dev(t=1 - self.t)]


def enter(place):
    barrier = pltpu.get_barrier_semaphore()
    peers = place.peers()
    for peer in peers:
        pl.semaphore_signal(barrier, inc=1, device_id=peer, device_id_type=MESH)
    pl.semaphore_wait(barrier, len(peers))


class Copy:
    def __init__(self, parts):
        self.parts = parts
        self.make().start()

    def make(self):
        src, dst, send, recv, device = self.parts()
        return pltpu.make_async_remote_copy(
            src_ref=src, dst_ref=dst, send_sem=send, recv_sem=recv, device_id=device, device_id_type=MESH
        )

    def wait_recv(self):
        self.make().wait_recv()

    def wait_send(self):
        self.make().wait_send()


def span(begin, width):
    return pl.ds(begin if isinstance(begin, int) else pl.multiple_of(begin, 128), width)


def cut(part, width):
    first = 256 if part == 0 or width == 512 else 128
    return ((0, first), (first, width - first))


class Gather:
    axes = (("y", "z"), ("z", "y"))

    def __init__(self, me, w, sems):
        self.me, self.w = me, w
        self.p0s, self.p0r, self.p1s, self.p1r, self.ss, self.sr = sems
        self.sibling = me.dev(c=1 - me.c)
        self.first, self.second, self.shared = {}, {}, {}

    def cols(self, group, part, piece=None):
        base, half, parts, _ = W_GROUPS[group]
        begin, width = parts[part]
        if piece is not None:
            more, width = cut(part, width)[piece]
            begin += more
        return span(self.me.c * half + (base + begin), width)

    def unit(self, group, part, step, piece=None):
        cols = self.cols(group, part, piece)
        if self.axes[part][1] == "y":
            return self.w.at[lax.rem(self.me.y + step, 4), :, :, cols]
        return self.w.at[:, lax.rem(self.me.z + step, 4), :, cols]

    def share(self, group, part, step):
        def parts():
            ref = self.unit(group, part, step)
            return ref, ref, self.ss.at[group, part, step], self.sr.at[group, part, step], self.sibling

        self.shared[group, part, step] = Copy(parts)

    def start(self, group):
        me = self.me
        for part in range(2):
            for step in (2, 1, 3):

                def parts(part=part, step=step):
                    at = (group, part, step - 1)
                    ref = self.w.at[me.y, me.z, :, self.cols(group, part)]
                    return ref, ref, self.p0s.at[at], self.p0r.at[at], me.ring(self.axes[part][0], step)

                self.first[group, part, step - 1] = Copy(parts)

    def onward(self, group, part, origin, piece, sem, step):
        def parts():
            ref, at = self.unit(group, part, origin, piece), (group, part, sem)
            return ref, ref, self.p1s.at[at], self.p1r.at[at], self.me.ring(self.axes[part][1], step)

        self.second[group, part, sem] = Copy(parts)

    def turn(self, group):
        for part in range(2):
            for step in (1, 3, 2):
                self.first[group, part, step - 1].wait_recv()
            for i, step in enumerate((1, 3)):
                self.onward(group, part, 0, None, i, step)
            self.share(group, part, 0)

    def forward(self, group):
        for part in range(2):
            for i, step in enumerate((1, 3)):
                self.second[group, part, i].wait_recv()
                self.onward(group, part, 4 - step, i, 2 + i, step)
                self.share(group, part, 4 - step)

    def finish(self, group):
        for part in range(2):
            for i in range(2):
                self.second[group, part, 2 + i].wait_recv()
            self.share(group, part, 2)

    def done(self, group):
        for part in range(2):
            for step in range(4):
                self.shared[group, part, step].wait_recv()

    def sent(self):
        for copies in (self.first, self.second, self.shared):
            for copy in copies.values():
                copy.wait_send()


class Reduce:
    axes = (("z", "y"), ("y", "z"))

    def __init__(self, me, g, land, ring1, ring2, red, sems):
        self.me, self.g, self.land, self.ring1, self.ring2, self.red = me, g, land, ring1, ring2, red
        self.cs, self.cr, self.p0s, self.p0r, self.p1s, self.p1r = sems
        self.sibling = me.dev(c=1 - me.c)
        self.pulled, self.first, self.second = {}, {}, {}

    def place(self, group, part, piece=None):
        _, _, parts, at = G_GROUPS[group]
        begin, width = parts[part]
        if piece is not None:
            more, width = cut(part, width)[piece]
            begin += more
        return begin, at + begin, width

    def unit(self, group, part, step, piece=None, core=None):
        base, half, _, _ = G_GROUPS[group]
        begin, _, width = self.place(group, part, piece)
        cols = span((self.me.c if core is None else core) * half + (base + begin), width)
        return self.of(self.g, part, step, cols)

    def of(self, ref, part, step, cols):
        if self.axes[part][0] == "y":
            return ref.at[lax.rem(self.me.y + step, 4), :, :, cols]
        return ref.at[:, lax.rem(self.me.z + step, 4), :, cols]

    def landed(self, group, part, step):
        _, at, width = self.place(group, part)
        return self.of(self.land, part, step, span(at, width))

    def add(self, dst, *terms):
        def body(i, carry):
            total = dst[i].astype(F32)
            for term in terms:
                total += term[i].astype(F32)
            dst[i] = total.astype(BF16)
            return carry

        lax.fori_loop(0, 4, body, 0)

    def pull(self, group, part):
        for step in (2, 1, 3, 0):

            def parts(step=step):
                at = (group, part, step)
                src = self.unit(group, part, step, core=1 - self.me.c)
                return src, self.landed(group, part, step), self.cs.at[at], self.cr.at[at], self.sibling

            self.pulled[group, part, step] = Copy(parts)

    def join(self, group, part, step):
        self.pulled[group, part, step].wait_recv()
        self.add(self.unit(group, part, step), self.landed(group, part, step))

    def piece1(self, group, part, i):
        _, at, width = self.place(group, part, i)
        return self.ring1.at[:, :, span(at, width)]

    def start(self, group):
        for part in range(2):
            self.join(group, part, 2)
            for i, step in enumerate((1, 3)):

                def parts(part=part, i=i, step=step):
                    at = (group, part, i)
                    src, dst = self.unit(group, part, 2, i), self.piece1(group, part, i)
                    return src, dst, self.p0s.at[at], self.p0r.at[at], self.me.ring(self.axes[part][0], step)

                self.first[group, part, i] = Copy(parts)

    def whole2(self, group, part, i):
        _, at, width = self.place(group, part)
        return self.ring2.at[i, :, :, span(at, width)]

    def turn(self, group):
        for part in range(2):
            for i, step in enumerate((1, 3)):
                self.join(group, part, step)
                self.first[group, part, i].wait_recv()
                self.add(self.unit(group, part, step, i), self.piece1(group, part, i))

                def parts(part=part, i=i, step=step):
                    at = (group, part, 2 + i)
                    src, dst = self.unit(group, part, step), self.whole2(group, part, i)
                    return src, dst, self.p0s.at[at], self.p0r.at[at], self.me.ring(self.axes[part][0], step)

                self.first[group, part, 2 + i] = Copy(parts)

    def across(self, group, part, step):
        me = self.me
        base, half, _, _ = G_GROUPS[group]
        begin, _, width = self.place(group, part)
        cols = span(me.c * half + (base + begin), width)
        if self.axes[part][1] == "y":
            return self.g.at[lax.rem(me.y + step, 4), me.z, :, cols]
        return self.g.at[me.y, lax.rem(me.z + step, 4), :, cols]

    def finish(self, group):
        for part in range(2):
            self.join(group, part, 0)
            for i in range(2):
                self.first[group, part, 2 + i].wait_recv()
            self.add(self.unit(group, part, 0), self.whole2(group, part, 0), self.whole2(group, part, 1))
            for step in (2, 1, 3):

                def parts(part=part, step=step):
                    _, at, width = self.place(group, part)
                    sem = (group, part, step - 1)
                    src, dst = self.across(group, part, step), self.red.at[step - 1, :, span(at, width)]
                    return src, dst, self.p1s.at[sem], self.p1r.at[sem], self.me.ring(self.axes[part][1], step)

                self.second[group, part, step - 1] = Copy(parts)

    def done(self, group, pick_t, quad):
        for part in range(2):
            _, at, width = self.place(group, part)
            total = self.across(group, part, 0)[...].astype(F32)
            for step in (1, 3, 2):
                self.second[group, part, step - 1].wait_recv()
                total += self.red[step - 1, :, at : at + width].astype(F32)
            quad[:, :, at : at + width] = nn(pick_t[...], total.astype(BF16)).astype(BF16).reshape(4, PAD, width)

    def sent(self):
        for copies in (self.pulled, self.first, self.second):
            for copy in copies.values():
                copy.wait_send()


def rotated(field, cosine, left, right, sign):
    n = field.shape[1]
    return field * cosine + sign * (pltpu.roll(field, n - 8, 1) * left + pltpu.roll(field, 8, 1) * right)


def kernel(
    mine, x, cot, perm, spread, mask, rows_at, rows_of, pick, pick_t, cos_t, left_t, right_t, start_col, start_row,
    out, grad, small_out, rows_out,
    w, g, land, ring1, ring2, red, quad_in, quad_out, quad_land, x_land, cot_land, out_send, out_land, nb_send, nb_land,
    small_mine, small_land,
    s1, s2, up, s1t, s2t, upt, hat, fac, q, k, v, cb, ctx, tb, act, ub, outp, sec, nbp, vec, gvec,
    ap0s, ap0r, ap1s, ap1r, ass, asr, rcs, rcr, rp0s, rp0r, rp1s, rp1r, qs, qr, ts, tr, es, er,
):
    me = Place()
    enter(me)
    partner = me.dev(t=1 - me.t)
    gather = Gather(me, w, (ap0s, ap0r, ap1s, ap1r, ass, asr))
    reduce = Reduce(me, g, land, ring1, ring2, red, (rcs, rcr, rp0s, rp0r, rp1s, rp1r))
    quads, swaps = [], []
    for r in (1, 2, 3):

        def parts(r=r):
            device, _, c = me.quad(r)
            return mine.at[c], quad_in.at[me.slot], qs.at[0, r], qr.at[0, r], device

        quads.append(Copy(parts))
    for i, (src, dst) in enumerate(((x, x_land), (cot, cot_land))):
        swaps.append(Copy(lambda src=src, dst=dst, i=i: (src, dst, ts.at[i], tr.at[i], partner)))
    quad_in[me.slot] = mine[me.c]
    gvec[...] = jnp.zeros_like(gvec)
    for copy in quads:
        copy.wait_recv()
    block = nn(pick[...], quad_in[...].reshape(64, WIDE)).astype(BF16)
    for base, half, _, at in W_GROUPS:
        w[me.y, me.z, :, span(me.c * half + base, half)] = block[:, at : at + half]
    gather.start(0)

    def norm_rows(x_ref, cot_ref, first_row):
        def body(i, carry):
            src = pl.ds(pl.multiple_of(i * 128, 128), 128)
            rows = pl.ds(pl.multiple_of(first_row + i * 128, 128), 128)
            field = nn(x_ref[src, :], perm[...])
            center = jnp.mean(field, axis=-1, keepdims=True)
            centred = field - center
            factor = lax.rsqrt(jnp.mean(centred * centred, axis=-1, keepdims=True) + EPSILON)
            hat[rows, :] = centred * factor
            fac[rows, :] = jnp.broadcast_to(factor, (128, 128))
            upstream = nn(cot_ref[src, :], perm[...])
            up[rows, :] = upstream.astype(BF16)
            upt[:, rows] = upstream.astype(BF16).T
            gvec[0:1, 4 * D : 5 * D] += jnp.sum(upstream, axis=0, keepdims=True)
            return carry

        lax.fori_loop(0, 2, body, 0)

    norm_rows(x, cot, me.t * HALF_T)
    gather.turn(0)
    gather.start(1)
    for copy in swaps:
        copy.wait_recv()
    norm_rows(x_land, cot_land, (1 - me.t) * HALF_T)
    gather.forward(0)
    gather.finish(0)
    gather.turn(1)
    gather.start(2)
    gather.done(0)

    def wcols(begin, width):
        return w[:, :, :, span(begin, width)].reshape(D, width)

    def wrows(i, begin, width):
        return w[2 * i : 2 * i + 2, :, :, begin : begin + width].reshape(384, width)

    def put(i, begin, value):
        width = value.shape[1]
        g[2 * i : 2 * i + 2, :, :, begin : begin + width] = value.astype(BF16).reshape(2, Z, BLK, width)

    small = nn(rows_of[...], wcols(W_SMALL, 128)).astype(BF16)
    for begin in range(0, VEC, D):
        width = min(D, VEC - begin)
        cols = slice(begin, begin + width)
        picked = nn(small, spread[:, cols]) * mask[:, cols].astype(F32)
        vec[:, cols] = jnp.broadcast_to(jnp.sum(picked, axis=0, keepdims=True), (8, width))

    def rowvec(begin, width):
        return vec[0:1, span(begin, width)]

    g0, g1, h0, h1, fb = (vec[0:1, i * D : (i + 1) * D] for i in range(5))

    def scale_rows(i, carry):
        rows = pl.ds(pl.multiple_of(i * 128, 128), 128)
        normal = hat[rows, :]
        first = (normal * g0 + h0).astype(BF16)
        second = (normal * g1 + h1).astype(BF16)
        s1[rows, :] = first
        s2[rows, :] = second
        s1t[:, rows] = first.T
        s2t[:, rows] = second.T
        return carry

    lax.fori_loop(0, 4, scale_rows, 0)

    def heads_in(i, carry):
        cols = span(i * 128, 128)
        for n, ref in enumerate((q, k, v)):
            field = nn(s1[...], wcols(n * 384 + i * 128, 128)) + rowvec(5 * D + n * 384 + i * 128, 128)
            if n < 2:
                field = rotated(field, cos_t[...], left_t[...], right_t[...], 1.0)
            ref[:, cols] = field.astype(BF16)
        cb[:, cols] = nn(up[...], wcols(W_DENSE + i * 128, 128)).astype(BF16)
        return carry

    lax.fori_loop(0, 3, heads_in, 0)
    gather.forward(1)

    scale = 1.0 / math.sqrt(HD)

    def attend(pair, carry):
        cols = span(pair * 128, 128)
        halves = []
        for head in range(2):
            inside = (lax.broadcasted_iota(jnp.int32, (1, 128), 1) // HD) == head
            grads_k, grads_v, outs, grads_q = [], [], [], []
            for block in range(2):
                begin, n = block * HALF_T, (block + 1) * HALF_T
                rows = slice(begin, begin + HALF_T)
                kk, vv = k[0:n, cols], v[0:n, cols]
                qq = jnp.where(inside, q[rows, cols], 0).astype(BF16)
                cc = jnp.where(inside, cb[rows, cols], 0).astype(BF16)
                place_t = begin + lax.broadcasted_iota(jnp.int32, (HALF_T, n), 0)
                place_s = lax.broadcasted_iota(jnp.int32, (HALF_T, n), 1)
                allowed = (start_col[rows, 0:1] == start_row[0:1, 0:n]) & (place_s <= place_t)
                scores = jnp.where(allowed, nt(qq, kk) * scale, -1e30)
                powers = jnp.exp(scores - jnp.max(scores, axis=-1, keepdims=True))
                probs = powers / jnp.sum(powers, axis=-1, keepdims=True)
                low = probs.astype(BF16)
                outs.append(nn(low, vv))
                back = nt(cc, vv)
                inner = jnp.sum(probs * back, axis=-1, keepdims=True)
                ds = (probs * (back - inner)).astype(BF16)
                grads_q.append(nn(ds, kk) * scale)
                grads_k.append(tn(ds, qq) * scale)
                grads_v.append(tn(low, cc))
            join = lambda parts: jnp.concatenate([parts[1][:HALF_T] + parts[0], parts[1][HALF_T:]], axis=0)
            halves.append(
                (jnp.concatenate(outs, axis=0), jnp.concatenate(grads_q, axis=0), join(grads_k), join(grads_v))
            )
        first = (lax.broadcasted_iota(jnp.int32, (1, 128), 1) // HD) == 0
        result, dq, dk, dv = (jnp.where(first, a, b) for a, b in zip(*halves))
        ctx[:, cols] = result.astype(BF16)
        for n, field in enumerate((dq, dk, dv)):
            if n < 2:
                field = rotated(field, cos_t[...], left_t[...], right_t[...], -1.0)
            field = field.astype(BF16)
            tb[:, span(n * 384 + pair * 128, 128)] = field
            gvec[0:1, span(5 * D + n * 384 + pair * 128, 128)] = jnp.sum(field.astype(F32), axis=0, keepdims=True)

        @pl.when(pair == 0)
        def _():
            gather.finish(1)
            gather.turn(2)

        @pl.when(pair == 1)
        def _():
            gather.forward(2)

        return carry

    lax.fori_loop(0, 3, attend, 0)
    gather.finish(2)

    for i in range(2):
        rows = slice(384 * i, 384 * i + 384)
        put(i, 0, nn(s1t[rows, :], tb[...]))
        put(i, G_DENSE, nn(upt[rows, :], ctx[...]))
    for part in range(2):
        reduce.pull(0, part)
    for i in range(2):
        rows = slice(384 * i, 384 * i + 384)
        outp[:, rows] = nt(ctx[...], wrows(i, W_DENSE, 384))
        first = nt(tb[...], wrows(i, 0, 1152))
        nbp[:, rows] = first * vec[0:1, rows]
        gvec[0:1, rows] = jnp.sum(first * hat[:, rows], axis=0, keepdims=True)
        gvec[0:1, slice(2 * D + 384 * i, 2 * D + 384 * i + 384)] = jnp.sum(first, axis=0, keepdims=True)
    gather.done(1)
    reduce.start(0)

    for half in range(2):
        base = W_UNITS[half]
        lane = 5 * D + 1152 + half * 768

        def units(i, carry, base=base, lane=lane):
            cols = span(i * 256, 256)
            pre = nn(s2[...], wcols(base + i * 256, 256)) + rowvec(lane + i * 256, 256)
            phi = 0.5 * (1.0 + lax.erf(pre * (1.0 / math.sqrt(2.0))))
            act[:, cols] = (pre * phi).astype(BF16)
            slope = phi + pre * jnp.exp(-0.5 * pre * pre) * (1.0 / math.sqrt(2.0 * math.pi))
            back = (nn(up[...], wcols(base + 768 + i * 256, 256)) * slope).astype(BF16)
            ub[:, cols] = back
            gvec[0:1, span(lane + i * 256, 256)] = jnp.sum(back.astype(F32), axis=0, keepdims=True)
            return carry

        lax.fori_loop(0, 3, units, 0)
        if half == 0:
            reduce.turn(0)
        else:
            reduce.done(0, pick_t, quad_out)
            reduce.turn(1)
        for i in range(2):
            rows = slice(384 * i, 384 * i + 384)
            put(i, G_INNER[half], nn(s2t[rows, :], ub[...]))
            put(i, G_OUTER[half], nn(upt[rows, :], act[...]))
        if half == 0:
            for part in range(2):
                reduce.pull(1, part)
        else:
            reduce.pull(2, 0)
        for i in range(2):
            rows = slice(384 * i, 384 * i + 384)
            outp[:, rows] += nt(act[...], wrows(i, base + 768, 768))
            second = nt(ub[...], wrows(i, base, 768))
            if half == 0:
                sec[:, rows] = second
            else:
                second += sec[:, rows]
                nbp[:, rows] += second * vec[0:1, D + 384 * i : D + 384 * i + 384]
                gvec[0:1, D + 384 * i : D + 384 * i + 384] = jnp.sum(second * hat[:, rows], axis=0, keepdims=True)
                gvec[0:1, 3 * D + 384 * i : 3 * D + 384 * i + 384] = jnp.sum(second, axis=0, keepdims=True)
        if half == 0:
            gather.done(2)
            reduce.finish(0)
            reduce.start(1)

    tile = jnp.zeros((64, 128), F32)
    for begin in range(0, VEC, D):
        width = min(D, VEC - begin)
        cols = slice(begin, begin + width)
        tile += nt((gvec[0:1, cols] * mask[:, cols].astype(F32)).astype(BF16), spread[:, cols])
    tile = nn(rows_at[...], tile.astype(BF16)).astype(BF16)
    g[:, :, :, G_SMALL : G_SMALL + 128] = tile.reshape(Y, Z, BLK, 128)
    g[:, :, :, COLS - 128 : COLS] = jnp.zeros((Y, Z, BLK, 128), BF16)
    reduce.pull(2, 1)
    reduce.start(2)

    own = me.t * HALF_T
    other = pl.ds(pl.multiple_of((1 - me.t) * HALF_T, HALF_T), HALF_T)
    out_send[...] = outp[other, :].astype(BF16)
    nb_send[...] = nbp[other, :].astype(BF16)
    for i, (src, dst) in enumerate(((out_send, out_land), (nb_send, nb_land))):
        swaps.append(Copy(lambda src=src, dst=dst, i=i: (src, dst, ts.at[2 + i], tr.at[2 + i], partner)))
    reduce.finish(1)
    reduce.turn(2)
    for copy in swaps[2:]:
        copy.wait_recv()

    def finish_rows(i, carry):
        rows = pl.ds(pl.multiple_of(i * 64, 64), 64)
        mine_at = pl.ds(pl.multiple_of(own + i * 64, 64), 64)
        low = (nn(x[rows, :], perm[...]) + outp[mine_at, :] + out_land[rows, :].astype(F32) + fb).astype(BF16)
        out[rows, :] = nt(low, perm[...]).astype(BF16)
        back = nbp[mine_at, :] + nb_land[rows, :].astype(F32)
        normal = hat[mine_at, :]
        value = up[mine_at, :].astype(F32) + fac[mine_at, 0:1] * (
            back
            - jnp.mean(back, axis=-1, keepdims=True)
            - normal * jnp.mean(back * normal, axis=-1, keepdims=True)
        )
        grad[rows, :] = nt(value.astype(BF16), perm[...]).astype(BF16)
        return carry

    lax.fori_loop(0, 4, finish_rows, 0)
    reduce.done(1, pick_t, quad_out)
    reduce.finish(2)
    reduce.done(2, pick_t, quad_out)
    owners = []
    for r in (1, 2, 3):

        def parts(r=r):
            device, xh, c = me.quad(r)
            return quad_out.at[xh * 2 + c], quad_land.at[me.slot], qs.at[1, r], qr.at[1, r], device

        owners.append(Copy(parts))
    quad_land[me.slot] = quad_out[me.slot]
    for copy in owners:
        copy.wait_recv()
    small_mine[...] = quad_land[0, :, WIDE - 128 :].astype(F32) + quad_land[2, :, WIDE - 128 :].astype(F32)
    last = Copy(lambda: (small_mine, small_land, es, er, partner))
    for c in range(2):
        rows_out[c] = quad_land[c].astype(F32) + quad_land[2 + c].astype(F32)
    for copy in quads + swaps + owners:
        copy.wait_send()
    gather.sent()
    reduce.sent()
    last.wait_send()
    last.wait_recv()
    lane = lax.broadcasted_iota(jnp.int32, (PAD, 128), 1)
    small_out[...] = small_mine[...] + jnp.where(lane < 4 * OWN, small_land[...], 0.0)


def turn_tables(starts):
    places = (jnp.arange(T, dtype=jnp.int32) - starts).astype(F32)
    lane = jnp.arange(128, dtype=jnp.int32) % HD
    freqs = jnp.exp((lane % 8).astype(F32) * (-2.0 * math.log(10000.0) / ROT))
    turns = places[:, None] * freqs[None, :]
    cosine, sine = jnp.cos(turns), jnp.sin(turns)
    return (
        jnp.where(lane < ROT, cosine, 1.0),
        jnp.where(lane < 8, -sine, 0.0),
        jnp.where((lane >= 8) & (lane < ROT), sine, 0.0),
    )


def local(
    layer_input, segment_starts, norm_gains, norm_shifts, projection, triple_bias, dense_weight, inner_weight,
    unit_bias, outer_weight, final_bias, cotangent,
):
    small = jnp.concatenate(
        [norm_gains.reshape(-1), norm_shifts.reshape(-1), final_bias, triple_bias.reshape(-1), unit_bias]
    )
    small = jnp.pad(small[None, :], ((0, OWN - 1), (0, 128 - small.shape[0])))
    triple = projection.reshape(OWN, 1152)
    mine = jnp.concatenate(
        [triple[:, :896], inner_weight, triple[:, 896:], small, dense_weight.T, jnp.zeros((OWN, 128), BF16), outer_weight.T],
        axis=1,
    )
    mine = jnp.pad(mine, ((0, PAD - OWN), (0, 0)))
    mine = jnp.stack([mine[:, :WIDE], mine[:, WIDE:]])
    start_col = jnp.broadcast_to(segment_starts[:, None], (T, 128))
    start_row = jnp.broadcast_to(segment_starts[None, :], (8, T))
    vm = pl.BlockSpec(memory_space=pltpu.VMEM)
    dma = pltpu.SemaphoreType.DMA
    struct = jax.ShapeDtypeStruct
    vmem = pltpu.VMEM
    out, grad, small_grad, rows_grad = pl.pallas_call(
        kernel,
        out_shape=(
            struct((HALF_T, D), BF16), struct((HALF_T, D), BF16), struct((PAD, 128), F32), struct((2, PAD, WIDE), F32),
        ),
        in_specs=[vm] * 15,
        out_specs=(vm,) * 4,
        scratch_shapes=[
            vmem((Y, Z, BLK, COLS), BF16), vmem((Y, Z, BLK, COLS), BF16), vmem((Y, Z, BLK, WIDE), BF16),
            vmem((4, BLK, WIDE), BF16), vmem((2, 4, BLK, WIDE), BF16), vmem((3, BLK, WIDE), BF16),
            vmem((4, PAD, WIDE), BF16), vmem((4, PAD, WIDE), BF16), vmem((4, PAD, WIDE), BF16),
        ]
        + [vmem((HALF_T, D), BF16)] * 6
        + [vmem((PAD, 128), F32)] * 2
        + [vmem((T, D), BF16)] * 3
        + [vmem((D, T), BF16)] * 3
        + [vmem((T, D), F32), vmem((T, 128), F32)]
        + [vmem((T, 384), BF16)] * 5
        + [vmem((T, 1152), BF16), vmem((T, 768), BF16), vmem((T, 768), BF16)]
        + [vmem((T, D), F32)] * 3
        + [vmem((8, VEC), F32)] * 2
        + [dma((3, 2, 3))] * 2
        + [dma((3, 2, 4))] * 4
        + [dma((3, 2, 4))] * 4
        + [dma((3, 2, 3))] * 2
        + [dma((2, 4))] * 2
        + [dma((4,))] * 2
        + [dma] * 2,
        compiler_params=pltpu.CompilerParams(collective_id=0, has_side_effects=True, vmem_limit_bytes=VMEM_LIMIT),
        name="layer",
    )(
        mine, layer_input, cotangent, *[jnp.asarray(m) for m in order_tables()], *turn_tables(segment_starts),
        start_col, start_row,
    )

    vals = small_grad[0]
    side = lax.axis_index("tensor")

    def six(field):
        return lax.dynamic_slice_in_dim(field, side * 6, 6, axis=field.ndim - 1)

    a, b = rows_grad[0, :OWN], rows_grad[1, :OWN]
    return (
        out,
        grad,
        six(vals[0:24].reshape(2, OWN)),
        six(vals[24:48].reshape(2, OWN)),
        jnp.concatenate([a[:, :768], b[:, :384]], axis=1).reshape(OWN, 3, 384),
        vals[OFF_TB:OFF_UB].reshape(3, 6),
        b[:, 384:768].T,
        a[:, 768:2304],
        vals[OFF_UB : OFF_UB + 24],
        b[:, 768:2304].T,
        six(vals[48:60]),
    )


def solution(mesh):
    placed = (
        P(("dp", "tensor"), None),
        P("dp"),
        P(None, "dp"),
        P(None, "dp"),
        P("dp", None, "tensor"),
        P(None, ("tensor", "dp")),
        P("tensor", "dp"),
        P("dp", "tensor"),
        P(("tensor", "dp")),
        P("tensor", "dp"),
        P("dp"),
        P(("dp", "tensor"), None),
    )
    return jax.shard_map(
        local,
        mesh=mesh,
        in_specs=placed,
        out_specs=(
            P(("dp", "tensor"), None),
            P(("dp", "tensor"), None),
            P(None, ("dp", "tensor")),
            P(None, ("dp", "tensor")),
            P("dp", None, "tensor"),
            P(None, ("tensor", "dp")),
            P("tensor", "dp"),
            P("dp", "tensor"),
            P(("tensor", "dp")),
            P("tensor", "dp"),
            P(("dp", "tensor")),
        ),
        check_vma=False,
    )
```

```python
import math

import jax
import jax.numpy as jnp
import numpy as np
from jax import lax
from jax.experimental import pallas as pl
from jax.experimental.pallas import tpu as pltpu
from jax.sharding import PartitionSpec as P

MESH = pl.DeviceIdType.MESH
F32, BF16 = jnp.float32, jnp.bfloat16

D, HD, ROT = 768, 64, 16
T, HALF_T = 512, 256
EPSILON = 1e-05
Y, XH, Z, CORE = 4, 2, 4, 2
OWN = 12
PAD = 16
BLK = OWN * XH * CORE
COLS, WIDE = 4864, 2432
W_SMALL, W_DENSE, W_UNITS = 1152, 1280, (1792, 3328)
G_COLS, G_WIDE = 4608, 2304
G_DENSE, G_INNER, G_OUTER = 1152, (1536, 3072), (2304, 3840)
EVEN = ((0, 384), (384, 384))
UNEVEN = ((0, 512), (512, 384))
W_GROUPS = ((0, 896, UNEVEN, 0), (1792, 768, EVEN, 896), (3328, 768, EVEN, 1664))
G_GROUPS = ((0, 768, EVEN, 0), (1536, 768, EVEN, 768), (3072, 768, EVEN, 1536))
VEC = 5 * D + 3 * 384 + 1536
OFF_TB, OFF_UB = 5 * OWN, 5 * OWN + 18
VMEM_LIMIT = 56 * 1024 * 1024


def order_tables():
    j = np.arange(64)
    c, xh, z, y = j % 2, (j // 2) % 2, (j // 4) % 4, j // 16
    dp = ((y * 2 + xh) * 4 + z) * 2 + c
    at = (12 * dp[:, None] + np.arange(12)[None, :]).reshape(-1)
    perm = np.zeros((D, D), np.float32)
    perm[at, np.arange(D)] = 1
    spread = np.zeros((128, VEC), np.float32)
    mask = np.zeros((64, VEC), np.float32)
    col = np.arange(D)
    for v in range(5):
        spread[v * 12 + col % 12, v * D + col] = 1
        mask[col // 12, v * D + col] = 1
    back = np.argsort(dp)
    col = np.arange(384)
    for k in range(3):
        spread[OFF_TB + 6 * k + col % 6, 5 * D + 384 * k + col] = 1
        mask[back[col // 6], 5 * D + 384 * k + col] = 1
    col = np.arange(1536)
    spread[OFF_UB + col % 24, 5 * D + 1152 + col] = 1
    mask[back[col // 24], 5 * D + 1152 + col] = 1
    rows = np.zeros((D, 64), np.float32)
    rows[12 * j, j] = 1
    eights = np.zeros((128, 64), np.float32)
    eights[8 * (j // 4) + j % 4, j] = 1
    pick = np.zeros((BLK, 64), np.float32)
    r = np.arange(BLK)
    pick[r, 16 * (r // 12) + r % 12] = 1
    return [m.astype(jnp.bfloat16) for m in (perm, spread, mask, eights, np.ascontiguousarray(rows.T), pick, np.ascontiguousarray(pick.T))]


def nn(a, b):
    return lax.dot_general(a, b, (((1,), (0,)), ((), ())), preferred_element_type=F32)


def nt(a, b):
    return lax.dot_general(a, b, (((1,), (1,)), ((), ())), preferred_element_type=F32)


def tn(a, b):
    return lax.dot_general(a, b, (((0,), (0,)), ((), ())), preferred_element_type=F32)


class Place:
    def __init__(self):
        dp = lax.axis_index("dp")
        self.t = lax.axis_index("tensor")
        self.c = lax.rem(dp, 2)
        self.z = lax.rem(lax.div(dp, 2), 4)
        self.xh = lax.rem(lax.div(dp, 8), 2)
        self.y = lax.div(dp, 16)
        self.slot = self.xh * 2 + self.c

    def dev(self, y=None, xh=None, z=None, c=None, t=None):
        y = self.y if y is None else y
        xh = self.xh if xh is None else xh
        z = self.z if z is None else z
        c = self.c if c is None else c
        t = self.t if t is None else t
        return (((y * 2 + xh) * 4 + z) * 2 + c, t)

    def ring(self, axis, step):
        at = lax.rem((self.y if axis == "y" else self.z) + step, 4)
        return self.dev(y=at) if axis == "y" else self.dev(z=at)

    def quad(self, r):
        c = 1 - self.c if r & 1 else self.c
        xh = 1 - self.xh if r & 2 else self.xh
        return self.dev(xh=xh, c=c), xh, c

    def other(self, r):
        c = 1 - self.c if r & 1 else self.c
        xh = 1 - self.xh if r & 2 else self.xh
        return self.dev(xh=xh, c=c, t=1 - self.t)

    def peers(self):
        out = [self.quad(r)[0] for r in (1, 2, 3)]
        for axis in ("y", "z"):
            out += [self.ring(axis, step) for step in (1, 2, 3)]
        return out + [self.other(r) for r in range(4)]


def enter(place):
    barrier = pltpu.get_barrier_semaphore()
    peers = place.peers()
    for peer in peers:
        pl.semaphore_signal(barrier, inc=1, device_id=peer, device_id_type=MESH)
    pl.semaphore_wait(barrier, len(peers))


class Copy:
    def __init__(self, parts):
        self.parts = parts
        self.make().start()

    def make(self):
        src, dst, send, recv, device = self.parts()
        return pltpu.make_async_remote_copy(
            src_ref=src, dst_ref=dst, send_sem=send, recv_sem=recv, device_id=device, device_id_type=MESH
        )

    def wait_recv(self):
        self.make().wait_recv()

    def wait_send(self):
        self.make().wait_send()


def span(begin, width):
    return pl.ds(begin if isinstance(begin, int) else pl.multiple_of(begin, 128), width)


def cut(part, width):
    first = 256 if part == 0 or width == 512 else 128
    return ((0, first), (first, width - first))


class Gather:
    axes = (("y", "z"), ("z", "y"))

    def __init__(self, me, w, sems):
        self.me, self.w = me, w
        self.p0s, self.p0r, self.p1s, self.p1r, self.ss, self.sr = sems
        self.sibling = me.dev(c=1 - me.c)
        self.first, self.second, self.shared = {}, {}, {}

    def cols(self, group, part, piece=None):
        base, half, parts, _ = W_GROUPS[group]
        begin, width = parts[part]
        if piece is not None:
            more, width = cut(part, width)[piece]
            begin += more
        return span(self.me.c * half + (base + begin), width)

    def unit(self, group, part, step, piece=None):
        cols = self.cols(group, part, piece)
        if self.axes[part][1] == "y":
            return self.w.at[lax.rem(self.me.y + step, 4), :, :, cols]
        return self.w.at[:, lax.rem(self.me.z + step, 4), :, cols]

    def share(self, group, part, step):
        def parts():
            ref = self.unit(group, part, step)
            return ref, ref, self.ss.at[group, part, step], self.sr.at[group, part, step], self.sibling

        self.shared[group, part, step] = Copy(parts)

    def start(self, group):
        me = self.me
        for part in range(2):
            for step in (2, 1, 3):

                def parts(part=part, step=step):
                    at = (group, part, step - 1)
                    ref = self.w.at[me.y, me.z, :, self.cols(group, part)]
                    return ref, ref, self.p0s.at[at], self.p0r.at[at], me.ring(self.axes[part][0], step)

                self.first[group, part, step - 1] = Copy(parts)

    def onward(self, group, part, origin, piece, sem, step):
        def parts():
            ref, at = self.unit(group, part, origin, piece), (group, part, sem)
            return ref, ref, self.p1s.at[at], self.p1r.at[at], self.me.ring(self.axes[part][1], step)

        self.second[group, part, sem] = Copy(parts)

    def turn(self, group):
        for part in range(2):
            for step in (1, 3, 2):
                self.first[group, part, step - 1].wait_recv()
            for i, step in enumerate((1, 3)):
                self.onward(group, part, 0, i, i, step)
            for i, step in enumerate((1, 3)):
                self.onward(group, part, 0, 1 - i, 4 + i, step)
            self.share(group, part, 0)

    def forward(self, group):
        for part in range(2):
            for i, step in enumerate((1, 3)):
                self.second[group, part, i].wait_recv()
                self.onward(group, part, 4 - step, i, 2 + i, step)

    def finish(self, group):
        for part in range(2):
            for i, step in enumerate((1, 3)):
                self.second[group, part, 4 + i].wait_recv()
                self.share(group, part, 4 - step)
        for part in range(2):
            for i in range(2):
                self.second[group, part, 2 + i].wait_recv()
            self.share(group, part, 2)

    def done(self, group):
        for part in range(2):
            for step in range(4):
                self.shared[group, part, step].wait_recv()

    def sent(self):
        for copies in (self.first, self.second, self.shared):
            for copy in copies.values():
                copy.wait_send()


class Reduce:
    axes = (("z", "y"), ("y", "z"))

    def __init__(self, me, g, land, ring1, ring2, red, sems):
        self.me, self.g, self.land, self.ring1, self.ring2, self.red = me, g, land, ring1, ring2, red
        self.cs, self.cr, self.p0s, self.p0r, self.p1s, self.p1r = sems
        self.sibling = me.dev(c=1 - me.c)
        self.pulled, self.first, self.second, self.delivered = {}, {}, {}, {}

    def place(self, group, part, piece=None):
        _, _, parts, at = G_GROUPS[group]
        begin, width = parts[part]
        if piece is not None:
            more, width = cut(part, width)[piece]
            begin += more
        return begin, at + begin, width

    def unit(self, group, part, step, piece=None, core=None):
        base, half, _, _ = G_GROUPS[group]
        begin, _, width = self.place(group, part, piece)
        cols = span((self.me.c if core is None else core) * half + (base + begin), width)
        return self.of(self.g, part, step, cols)

    def of(self, ref, part, step, cols):
        if self.axes[part][0] == "y":
            return ref.at[lax.rem(self.me.y + step, 4), :, :, cols]
        return ref.at[:, lax.rem(self.me.z + step, 4), :, cols]

    def landed(self, group, part, step):
        _, at, width = self.place(group, part)
        return self.of(self.land, part, step, span(at, width))

    def add(self, dst, *terms):
        def body(i, carry):
            total = dst[i].astype(F32)
            for term in terms:
                total += term[i].astype(F32)
            dst[i] = total.astype(BF16)
            return carry

        lax.fori_loop(0, 4, body, 0)

    def pull(self, group, part):
        for step in (2, 1, 3, 0):

            def parts(step=step):
                at = (group, part, step)
                src = self.unit(group, part, step, core=1 - self.me.c)
                return src, self.landed(group, part, step), self.cs.at[at], self.cr.at[at], self.sibling

            self.pulled[group, part, step] = Copy(parts)

    def join(self, group, part, step):
        self.pulled[group, part, step].wait_recv()
        self.add(self.unit(group, part, step), self.landed(group, part, step))

    def piece1(self, group, part, i):
        _, at, width = self.place(group, part, i)
        return self.ring1.at[:, :, span(at, width)]

    def start(self, group):
        for part in range(2):
            self.join(group, part, 2)
            for i, step in enumerate((1, 3)):

                def parts(part=part, i=i, step=step):
                    at = (group, part, i)
                    src, dst = self.unit(group, part, 2, i), self.piece1(group, part, i)
                    return src, dst, self.p0s.at[at], self.p0r.at[at], self.me.ring(self.axes[part][0], step)

                self.first[group, part, i] = Copy(parts)
        for part in range(2):
            for i, step in enumerate((1, 3)):
                self.join(group, part, step)
                self.owner(group, part, i, 1 - i, 4 + i, step)

    def owner(self, group, part, i, piece, sem, step):
        def parts():
            at = (group, part, sem)
            src, dst = self.unit(group, part, step, piece), self.whole2(group, part, i, piece)
            return src, dst, self.p0s.at[at], self.p0r.at[at], self.me.ring(self.axes[part][0], step)

        self.first[group, part, sem] = Copy(parts)

    def whole2(self, group, part, i, piece=None):
        _, at, width = self.place(group, part, piece)
        return self.ring2.at[i, :, :, span(at, width)]

    def turn(self, group):
        for part in range(2):
            for i, step in enumerate((1, 3)):
                self.first[group, part, i].wait_recv()
                self.add(self.unit(group, part, step, i), self.piece1(group, part, i))
                self.owner(group, part, i, i, 2 + i, step)

    def across(self, group, part, step):
        me = self.me
        base, half, _, _ = G_GROUPS[group]
        begin, _, width = self.place(group, part)
        cols = span(me.c * half + (base + begin), width)
        if self.axes[part][1] == "y":
            return self.g.at[lax.rem(me.y + step, 4), me.z, :, cols]
        return self.g.at[me.y, lax.rem(me.z + step, 4), :, cols]

    def finish(self, group):
        for part in range(2):
            self.join(group, part, 0)
            for i in range(2):
                self.first[group, part, 4 + i].wait_recv()
                self.first[group, part, 2 + i].wait_recv()
            self.add(self.unit(group, part, 0), self.whole2(group, part, 0), self.whole2(group, part, 1))
            for step in (2, 1, 3):

                def parts(part=part, step=step):
                    _, at, width = self.place(group, part)
                    sem = (group, part, step - 1)
                    src, dst = self.across(group, part, step), self.red.at[step - 1, :, span(at, width)]
                    return src, dst, self.p1s.at[sem], self.p1r.at[sem], self.me.ring(self.axes[part][1], step)

                self.second[group, part, step - 1] = Copy(parts)

    def done(self, group, pick_t, quad):
        for part in range(2):
            _, at, width = self.place(group, part)
            total = self.across(group, part, 0)[...].astype(F32)
            for step in (1, 3, 2):
                self.second[group, part, step - 1].wait_recv()
                total += self.red[step - 1, :, at : at + width].astype(F32)
            quad[:, :, at : at + width] = nn(pick_t[...], total.astype(BF16)).astype(BF16).reshape(4, PAD, width)

    def deliver(self, group, quad, landing, qs, qr):
        me = self.me
        _, half, _, at = G_GROUPS[group]
        for r in (1, 2, 3):

            def parts(r=r):
                device, xh, c = me.quad(r)
                src, dst = quad.at[xh * 2 + c, :, span(at, half)], landing.at[me.slot, :, span(at, half)]
                return src, dst, qs.at[1, group, r], qr.at[1, group, r], device

            self.delivered[group, r] = Copy(parts)
        landing[me.slot, :, at : at + half] = quad[me.slot, :, at : at + half]

    def sent(self):
        for copies in (self.pulled, self.first, self.second, self.delivered):
            for copy in copies.values():
                copy.wait_send()


class Small:
    def __init__(self, me, mine, land_z, land_y, land_q, sends, recvs):
        self.me, self.mine, self.land_z, self.land_y, self.land_q = me, mine, land_z, land_y, land_q
        self.sends, self.recvs, self.copies = sends, recvs, {}

    def copy(self, n, src, dst, device):
        self.copies[n] = Copy(lambda: (src(), dst(), self.sends.at[n], self.recvs.at[n], device()))

    def start(self):
        me = self.me
        for step in (2, 1, 3):
            self.copy(
                step - 1,
                lambda step=step: self.mine.at[:, lax.rem(me.z + step, 4)],
                lambda step=step: self.land_z.at[step - 1],
                lambda step=step: me.ring("z", step),
            )

    def turn(self):
        me = self.me
        for n in range(3):
            self.copies[n].wait_recv()
        self.land_z[3] = self.mine[:, me.z] + self.land_z[0] + self.land_z[1] + self.land_z[2]
        for step in (2, 1, 3):
            self.copy(
                2 + step,
                lambda step=step: self.land_z.at[3, lax.rem(me.y + step, 4)],
                lambda step=step: self.land_y.at[step - 1],
                lambda step=step: me.ring("y", step),
            )

    def finish(self):
        me = self.me
        for n in range(3):
            self.copies[3 + n].wait_recv()
        self.land_y[3] = self.land_z[3, me.y] + self.land_y[0] + self.land_y[1] + self.land_y[2]
        place = me.t * 4 + me.slot
        self.land_q[place] = self.land_y[3]
        for r in range(7):
            self.copy(
                6 + r,
                lambda: self.land_y.at[3],
                lambda: self.land_q.at[me.t * 4 + me.slot],
                lambda r=r: me.quad(r + 1)[0] if r < 3 else me.other(r - 3),
            )

    def done(self):
        me = self.me
        for r in range(7):
            self.copies[6 + r].wait_recv()
        lane = lax.broadcasted_iota(jnp.int32, (8, 128), 1)
        row = lax.broadcasted_iota(jnp.int32, (8, 128), 0)
        total = jnp.zeros((8, 128), F32)
        for n in range(4):
            total += self.land_q[me.t * 4 + n] + jnp.where(lane < 4 * OWN, self.land_q[(1 - me.t) * 4 + n], 0.0)
        return jnp.broadcast_to(jnp.sum(jnp.where(row == me.slot, total, 0.0), axis=0, keepdims=True), (8, 128))

    def sent(self):
        for copy in self.copies.values():
            copy.wait_send()


def rotated(field, cosine, left, right, sign):
    n = field.shape[1]
    return field * cosine + sign * (pltpu.roll(field, n - 8, 1) * left + pltpu.roll(field, 8, 1) * right)


def one_hot(shape, test):
    row = lax.broadcasted_iota(jnp.int32, shape, 0)
    col = lax.broadcasted_iota(jnp.int32, shape, 1)
    return jnp.where(test(row, col), 1.0, 0.0)


def pack(triple, dense, inner, outer, small, mine):
    mine[...] = jnp.zeros_like(mine)
    tall = one_hot((PAD, OWN), lambda r, c: r == c).astype(BF16)
    line = jnp.zeros((1, 128), F32)
    begin = 0
    for ref in small:
        count, width = ref.shape
        for i in range(count):
            put = one_hot((width, 128), lambda r, c, begin=begin: c == r + begin).astype(BF16)
            line += nn(ref[i : i + 1, :], put)
            begin += width
    first = lax.broadcasted_iota(jnp.int32, (PAD, 128), 0) == 0
    rows = nn(tall, triple[...]).astype(BF16)
    mine[0, :, 0:896] = rows[:, 0:896]
    mine[0, :, 896:WIDE] = nn(tall, inner[...]).astype(BF16)
    mine[1, :, 0:256] = rows[:, 896:1152]
    mine[1, :, 256:384] = jnp.where(first, line, 0.0).astype(BF16)
    mine[1, :, 384:768] = nn(tall, dense[...]).astype(BF16)
    mine[1, :, 896:WIDE] = nn(tall, outer[...]).astype(BF16)


def turn_tables(starts, cos_t, left_t, right_t, bias):
    begin = jnp.broadcast_to(starts[...].astype(F32), (8, T))
    places = lax.broadcasted_iota(jnp.int32, (8, T), 1).astype(F32) - begin
    freqs = jnp.exp(lax.broadcasted_iota(jnp.int32, (8, T), 0).astype(F32) * (-2.0 * math.log(10000.0) / ROT))
    turns = places * freqs

    def spread_lanes(rows, test):
        put = one_hot((8, 128), lambda r, c: (c % 8 == r) & test(c % HD))
        return lax.dot_general(
            rows.T, put, (((1,), (0,)), ((), ())), preferred_element_type=F32, precision=lax.Precision.HIGHEST
        )

    lane = lax.broadcasted_iota(jnp.int32, (1, 128), 1) % HD
    sine = jnp.sin(turns)
    cos_t[...] = spread_lanes(jnp.cos(turns), lambda c: c < ROT) + jnp.where(lane < ROT, 0.0, 1.0)
    left_t[...] = -spread_lanes(sine, lambda c: c < ROT // 2)
    right_t[...] = spread_lanes(sine, lambda c: (c >= ROT // 2) & (c < ROT))
    begin_col = begin.T[:, 0:1]

    def body(i, carry):
        rows = pl.ds(pl.multiple_of(i * 128, 128), 128)
        place_t = i * 128 + lax.broadcasted_iota(jnp.int32, (128, T), 0)
        place_s = lax.broadcasted_iota(jnp.int32, (128, T), 1)
        col = bias[rows, 0:1]
        bias[rows, :] = jnp.where((col == begin[0:1, :]) & (place_s <= place_t), 0.0, -1e30)
        return carry

    bias[:, 0:128] = jnp.broadcast_to(begin_col, (T, 128))
    lax.fori_loop(0, 4, body, 0)


def unpack_kernel(rows, small, gains, shifts, triple_b, units, final, proj, dense, inner, outer):
    side = lax.axis_index("tensor")
    line = jnp.broadcast_to(small[0:1, :], (8, 128))

    def lanes(begin, width):
        put = one_hot((128, width), lambda r, c: r == c + begin)
        picked = lax.dot_general(
            line, put, (((1,), (0,)), ((), ())), preferred_element_type=F32, precision=lax.Precision.HIGHEST
        )
        return picked[0:1, :]

    for i in range(2):
        gains[i : i + 1, :] = lanes(OWN * i + side * 6, 6)
        shifts[i : i + 1, :] = lanes(2 * OWN + OWN * i + side * 6, 6)
    for i in range(3):
        triple_b[i : i + 1, :] = lanes(OFF_TB + 6 * i, 6)
    units[...] = lanes(OFF_UB, 24)
    final[...] = lanes(4 * OWN + side * 6, 6)
    proj[:, 0:768] = rows[0, 0:OWN, 0:768]
    proj[:, 768:1152] = rows[1, 0:OWN, 0:384]
    inner[...] = rows[0, 0:OWN, 768:2304]
    dense[...] = rows[1, 0:OWN, 384:768]
    outer[...] = rows[1, 0:OWN, 768:2304]


def kernel(
    triple, dense, inner_w, outer_w, gains, shifts, fbias, tbias, ubias, starts, x, cot,
    perm, spread, mask, rows_at, rows_of, pick, pick_t,
    out, grad, small_out, rows_out,
    w, g, land, ring1, ring2, red, quad_in, quad_out, quad_land, x_land, cot_land, out_send, out_land, nb_send, nb_land,
    small_mine, small_z, small_y, small_q,
    s1, s2, up, s1t, s2t, upt, hat, fac, q, k, v, cb, ctx, tb, act, ub, outp, nbp, vec, gvec,
    mine, cos_t, left_t, right_t, bias, slope,
    ap0s, ap0r, ap1s, ap1r, ass, asr, rcs, rcr, rp0s, rp0r, rp1s, rp1r, qs, qr, ts, tr, es, er,
):
    me = Place()
    pack(triple, dense, inner_w, outer_w, (gains, shifts, fbias, tbias, ubias), mine)
    enter(me)
    partner = me.dev(t=1 - me.t)
    gather = Gather(me, w, (ap0s, ap0r, ap1s, ap1r, ass, asr))
    reduce = Reduce(me, g, land, ring1, ring2, red, (rcs, rcr, rp0s, rp0r, rp1s, rp1r))
    minor = Small(me, small_mine, small_z, small_y, small_q, es, er)
    quads, swaps = {}, []
    for group, (_, half, _, at) in enumerate(W_GROUPS):
        for r in (1, 2, 3):

            def parts(group=group, half=half, at=at, r=r):
                device, _, c = me.quad(r)
                src, dst = mine.at[c, :, span(at, half)], quad_in.at[me.slot, :, span(at, half)]
                return src, dst, qs.at[0, group, r], qr.at[0, group, r], device

            quads[group, r] = Copy(parts)

    def swap(i, src, dst):
        swaps.append(Copy(lambda: (src, dst, ts.at[i], tr.at[i], partner)))

    quad_in[me.slot] = mine[me.c]
    gvec[...] = jnp.zeros_like(gvec)
    turn_tables(starts, cos_t, left_t, right_t, bias)
    swap(0, x, x_land)

    def block(group):
        base, half, _, at = W_GROUPS[group]
        for r in (1, 2, 3):
            quads[group, r].wait_recv()
        rows = quad_in[:, :, at : at + half].reshape(64, half)
        w[me.y, me.z, :, span(me.c * half + base, half)] = nn(pick[...], rows).astype(BF16)
        gather.start(group)

    block(0)
    swap(1, cot, cot_land)
    def norm_rows(x_ref, first_row):
        def body(i, carry):
            src = pl.ds(pl.multiple_of(i * 128, 128), 128)
            rows = pl.ds(pl.multiple_of(first_row + i * 128, 128), 128)
            field = nn(x_ref[src, :], perm[...])
            center = jnp.mean(field, axis=-1, keepdims=True)
            centred = field - center
            factor = lax.rsqrt(jnp.mean(centred * centred, axis=-1, keepdims=True) + EPSILON)
            hat[rows, :] = centred * factor
            fac[rows, :] = jnp.broadcast_to(factor, (128, 128))
            return carry

        lax.fori_loop(0, 2, body, 0)

    def back_rows(cot_ref, first_row):
        def body(i, carry):
            src = pl.ds(pl.multiple_of(i * 128, 128), 128)
            rows = pl.ds(pl.multiple_of(first_row + i * 128, 128), 128)
            upstream = nn(cot_ref[src, :], perm[...])
            up[rows, :] = upstream.astype(BF16)
            upt[:, rows] = upstream.astype(BF16).T
            gvec[0:1, 4 * D : 5 * D] += jnp.sum(upstream, axis=0, keepdims=True)
            return carry

        lax.fori_loop(0, 2, body, 0)

    norm_rows(x, me.t * HALF_T)
    gather.turn(0)
    back_rows(cot, me.t * HALF_T)
    block(1)
    gather.forward(0)
    swaps[0].wait_recv()
    norm_rows(x_land, (1 - me.t) * HALF_T)
    gather.finish(0)
    gather.turn(1)
    block(2)
    gather.done(0)

    def wcols(begin, width):
        return w[:, :, :, span(begin, width)].reshape(D, width)

    def wrows(i, begin, width):
        return w[2 * i : 2 * i + 2, :, :, begin : begin + width].reshape(384, width)

    def put(i, begin, value):
        width = value.shape[1]
        g[2 * i : 2 * i + 2, :, :, begin : begin + width] = value.astype(BF16).reshape(2, Z, BLK, width)

    small = nn(rows_of[...], wcols(W_SMALL, 128)).astype(BF16)
    for begin in range(0, VEC, D):
        width = min(D, VEC - begin)
        cols = slice(begin, begin + width)
        picked = nn(small, spread[:, cols]) * mask[:, cols].astype(F32)
        vec[:, cols] = jnp.broadcast_to(jnp.sum(picked, axis=0, keepdims=True), (8, width))

    def rowvec(begin, width):
        return vec[0:1, span(begin, width)]

    g0, g1, h0, h1, fb = (vec[0:1, i * D : (i + 1) * D] for i in range(5))

    def scale_rows(i, carry):
        rows = pl.ds(pl.multiple_of(i * 128, 128), 128)
        normal = hat[rows, :]
        first = (normal * g0 + h0).astype(BF16)
        second = (normal * g1 + h1).astype(BF16)
        s1[rows, :] = first
        s2[rows, :] = second
        s1t[:, rows] = first.T
        s2t[:, rows] = second.T
        return carry

    lax.fori_loop(0, 4, scale_rows, 0)
    swaps[1].wait_recv()
    back_rows(cot_land, (1 - me.t) * HALF_T)

    scale = 1.0 / math.sqrt(HD)

    def heads_in(i, carry):
        cols = span(i * 128, 128)
        for n, ref in enumerate((q, k, v)):
            field = nn(s1[...], wcols(n * 384 + i * 128, 128)) + rowvec(5 * D + n * 384 + i * 128, 128)
            if n < 2:
                field = rotated(field, cos_t[...], left_t[...], right_t[...], 1.0)
            field = field.astype(BF16)
            ref[:, cols] = field * BF16(scale) if n == 0 else field
        cb[:, cols] = nn(up[...], wcols(W_DENSE + i * 128, 128)).astype(BF16)
        return carry

    lax.fori_loop(0, 3, heads_in, 0)
    gather.forward(1)

    def attend(pair, carry):
        cols = span(pair * 128, 128)
        halves = []
        for head in range(2):
            inside = (lax.broadcasted_iota(jnp.int32, (1, 128), 1) // HD) == head
            grads_k, grads_v, outs, grads_q = [], [], [], []
            for block in range(2):
                begin, n = block * HALF_T, (block + 1) * HALF_T
                rows = slice(begin, begin + HALF_T)
                kk, vv = k[0:n, cols], v[0:n, cols]
                qq = jnp.where(inside, q[rows, cols], 0).astype(BF16)
                cc = jnp.where(inside, cb[rows, cols], 0).astype(BF16)
                scores = nt(qq, kk) + bias[rows, 0:n]
                powers = jnp.exp(scores - jnp.max(scores, axis=-1, keepdims=True))
                probs = powers * (1.0 / jnp.sum(powers, axis=-1, keepdims=True))
                low = probs.astype(BF16)
                outs.append(nn(low, vv))
                back = nt(cc, vv)
                inner = jnp.sum(probs * back, axis=-1, keepdims=True)
                ds = (probs * (back - inner)).astype(BF16)
                grads_q.append(nn(ds, kk) * scale)
                grads_k.append(tn(ds, qq))
                grads_v.append(tn(low, cc))
            join = lambda parts: jnp.concatenate([parts[1][:HALF_T] + parts[0], parts[1][HALF_T:]], axis=0)
            halves.append(
                (jnp.concatenate(outs, axis=0), jnp.concatenate(grads_q, axis=0), join(grads_k), join(grads_v))
            )
        first = (lax.broadcasted_iota(jnp.int32, (1, 128), 1) // HD) == 0
        result, dq, dk, dv = (jnp.where(first, a, b) for a, b in zip(*halves))
        ctx[:, cols] = result.astype(BF16)
        for n, field in enumerate((dq, dk, dv)):
            if n < 2:
                field = rotated(field, cos_t[...], left_t[...], right_t[...], -1.0)
            field = field.astype(BF16)
            tb[:, span(n * 384 + pair * 128, 128)] = field
            gvec[0:1, span(5 * D + n * 384 + pair * 128, 128)] = jnp.sum(field.astype(F32), axis=0, keepdims=True)

        @pl.when(pair == 0)
        def _():
            gather.finish(1)
            gather.turn(2)

        @pl.when(pair == 1)
        def _():
            gather.forward(2)

        return carry

    lax.fori_loop(0, 3, attend, 0)
    gather.finish(2)

    for i in range(2):
        rows = slice(384 * i, 384 * i + 384)
        put(i, 0, nn(s1t[rows, :], tb[...]))
        put(i, G_DENSE, nn(upt[rows, :], ctx[...]))
    for part in range(2):
        reduce.pull(0, part)
    for i in range(2):
        rows = slice(384 * i, 384 * i + 384)
        outp[:, rows] = nt(ctx[...], wrows(i, W_DENSE, 384))
        first = nt(tb[...], wrows(i, 0, 1152))
        nbp[:, rows] = first * vec[0:1, rows]
        gvec[0:1, rows] = jnp.sum(first * hat[:, rows], axis=0, keepdims=True)
        gvec[0:1, slice(2 * D + 384 * i, 2 * D + 384 * i + 384)] = jnp.sum(first, axis=0, keepdims=True)
    gather.done(1)
    reduce.start(0)

    own = me.t * HALF_T
    other = pl.ds(pl.multiple_of((1 - me.t) * HALF_T, HALF_T), HALF_T)

    def units(half):
        def body(i, carry):
            cols = span(half * 768 + i * 256, 256)
            lane = 5 * D + 1152 + half * 768 + i * 256
            pre = nn(s2[...], wcols(W_UNITS[half] + i * 256, 256)) + rowvec(lane, 256)
            phi = 0.5 * (1.0 + lax.erf(pre * (1.0 / math.sqrt(2.0))))
            act[:, cols] = (pre * phi).astype(BF16)
            slope[:, cols] = phi + pre * jnp.exp(-0.5 * pre * pre) * (1.0 / math.sqrt(2.0 * math.pi))
            return carry

        lax.fori_loop(0, 3, body, 0)

    def units_back(half):
        def body(i, carry):
            cols = span(half * 768 + i * 256, 256)
            back = (nn(up[...], wcols(W_UNITS[half] + 768 + i * 256, 256)) * slope[:, cols]).astype(BF16)
            ub[:, cols] = back
            lane = 5 * D + 1152 + half * 768 + i * 256
            gvec[0:1, span(lane, 256)] = jnp.sum(back.astype(F32), axis=0, keepdims=True)
            return carry

        lax.fori_loop(0, 3, body, 0)

    def grads(half):
        cols = slice(768 * half, 768 * half + 768)
        for i in range(2):
            rows = slice(384 * i, 384 * i + 384)
            put(i, G_INNER[half], nn(s2t[rows, :], ub[:, cols]))
            put(i, G_OUTER[half], nn(upt[rows, :], act[:, cols]))
        for part in range(2):
            reduce.pull(1 + half, part)

    units(0)
    reduce.turn(0)
    gather.done(2)
    units(1)
    for i in range(2):
        rows = slice(384 * i, 384 * i + 384)
        outp[:, rows] += nt(act[:, 0:768], wrows(i, W_UNITS[0] + 768, 768))
        outp[:, rows] += nt(act[:, 768:1536], wrows(i, W_UNITS[1] + 768, 768))
    out_send[...] = outp[other, :].astype(BF16)
    swap(2, out_send, out_land)
    reduce.finish(0)
    units_back(0)
    grads(0)
    units_back(1)
    reduce.start(1)
    grads(1)
    reduce.done(0, pick_t, quad_out)
    reduce.deliver(0, quad_out, quad_land, qs, qr)
    reduce.turn(1)
    for i in range(2):
        rows = slice(384 * i, 384 * i + 384)
        second = nt(ub[:, 0:768], wrows(i, W_UNITS[0], 768)) + nt(ub[:, 768:1536], wrows(i, W_UNITS[1], 768))
        nbp[:, rows] += second * vec[0:1, D + 384 * i : D + 384 * i + 384]
        gvec[0:1, D + 384 * i : D + 384 * i + 384] = jnp.sum(second * hat[:, rows], axis=0, keepdims=True)
        gvec[0:1, 3 * D + 384 * i : 3 * D + 384 * i + 384] = jnp.sum(second, axis=0, keepdims=True)
    nb_send[...] = nbp[other, :].astype(BF16)
    swap(3, nb_send, nb_land)
    reduce.start(2)
    tile = jnp.zeros((64, 128), F32)
    for begin in range(0, VEC, D):
        width = min(D, VEC - begin)
        cols = slice(begin, begin + width)
        tile += nt((gvec[0:1, cols] * mask[:, cols].astype(F32)).astype(BF16), spread[:, cols])
    small_mine[...] = nn(rows_at[...], tile.astype(BF16)).reshape(Y, Z, 8, 128)
    minor.start()
    reduce.finish(1)
    reduce.turn(2)
    minor.turn()
    reduce.done(1, pick_t, quad_out)
    reduce.deliver(1, quad_out, quad_land, qs, qr)
    minor.finish()
    reduce.finish(2)
    for copy in swaps[2:]:
        copy.wait_recv()

    def finish_rows(i, carry):
        rows = pl.ds(pl.multiple_of(i * 64, 64), 64)
        mine_at = pl.ds(pl.multiple_of(own + i * 64, 64), 64)
        low = (nn(x[rows, :], perm[...]) + outp[mine_at, :] + out_land[rows, :].astype(F32) + fb).astype(BF16)
        out[rows, :] = nt(low, perm[...]).astype(BF16)
        back = nbp[mine_at, :] + nb_land[rows, :].astype(F32)
        normal = hat[mine_at, :]
        value = up[mine_at, :].astype(F32) + fac[mine_at, 0:1] * (
            back
            - jnp.mean(back, axis=-1, keepdims=True)
            - normal * jnp.mean(back * normal, axis=-1, keepdims=True)
        )
        grad[rows, :] = nt(value.astype(BF16), perm[...]).astype(BF16)
        return carry

    lax.fori_loop(0, 4, finish_rows, 0)
    reduce.done(2, pick_t, quad_out)
    reduce.deliver(2, quad_out, quad_land, qs, qr)
    small_out[...] = minor.done()
    for copy in reduce.delivered.values():
        copy.wait_recv()
    for c in range(2):
        rows_out[c] = quad_land[c].astype(F32) + quad_land[2 + c].astype(F32)
    for copy in list(quads.values()) + swaps:
        copy.wait_send()
    gather.sent()
    reduce.sent()
    minor.sent()


def local(
    layer_input, segment_starts, norm_gains, norm_shifts, projection, triple_bias, dense_weight, inner_weight,
    unit_bias, outer_weight, final_bias, cotangent,
):
    vm = pl.BlockSpec(memory_space=pltpu.VMEM)
    dma = pltpu.SemaphoreType.DMA
    struct = jax.ShapeDtypeStruct
    vmem = pltpu.VMEM
    out, grad, small_grad, rows_grad = pl.pallas_call(
        kernel,
        out_shape=(
            struct((HALF_T, D), BF16), struct((HALF_T, D), BF16), struct((8, 128), F32), struct((2, PAD, G_WIDE), F32),
        ),
        in_specs=[vm] * 19,
        out_specs=(vm,) * 4,
        scratch_shapes=[
            vmem((Y, Z, BLK, COLS), BF16), vmem((Y, Z, BLK, G_COLS), BF16), vmem((Y, Z, BLK, G_WIDE), BF16),
            vmem((4, BLK, G_WIDE), BF16), vmem((2, 4, BLK, G_WIDE), BF16), vmem((3, BLK, G_WIDE), BF16),
            vmem((4, PAD, WIDE), BF16), vmem((4, PAD, G_WIDE), BF16), vmem((4, PAD, G_WIDE), BF16),
        ]
        + [vmem((HALF_T, D), BF16)] * 6
        + [vmem((Y, Z, 8, 128), F32), vmem((4, 4, 8, 128), F32), vmem((4, 8, 128), F32), vmem((8, 8, 128), F32)]
        + [vmem((T, D), BF16)] * 3
        + [vmem((D, T), BF16)] * 3
        + [vmem((T, D), F32), vmem((T, 128), F32)]
        + [vmem((T, 384), BF16)] * 5
        + [vmem((T, 1152), BF16), vmem((T, 1536), BF16), vmem((T, 1536), BF16)]
        + [vmem((T, D), F32)] * 2
        + [vmem((8, VEC), F32)] * 2
        + [vmem((2, PAD, WIDE), BF16)]
        + [vmem((T, 128), F32)] * 3
        + [vmem((T, T), F32), vmem((T, 1536), F32)]
        + [dma((3, 2, 3))] * 2
        + [dma((3, 2, 6))] * 2
        + [dma((3, 2, 4))] * 4
        + [dma((3, 2, 6))] * 2
        + [dma((3, 2, 3))] * 2
        + [dma((2, 3, 4))] * 2
        + [dma((4,))] * 2
        + [dma((13,))] * 2,
        compiler_params=pltpu.CompilerParams(collective_id=0, has_side_effects=True, vmem_limit_bytes=VMEM_LIMIT),
        name="layer",
    )(
        projection.reshape(OWN, 1152), dense_weight.T, inner_weight, outer_weight.T, norm_gains, norm_shifts,
        final_bias.reshape(1, OWN), triple_bias, unit_bias.reshape(1, 24), segment_starts.reshape(1, T),
        layer_input, cotangent, *[jnp.asarray(m) for m in order_tables()],
    )
    gains, shifts, triple_b, units, final, proj, dense, inner, outer = pl.pallas_call(
        unpack_kernel,
        out_shape=(
            struct((2, 6), F32), struct((2, 6), F32), struct((3, 6), F32), struct((1, 24), F32), struct((1, 6), F32),
            struct((OWN, 1152), F32), struct((OWN, 384), F32), struct((OWN, 1536), F32), struct((OWN, 1536), F32),
        ),
        in_specs=[vm] * 2,
        out_specs=(vm,) * 9,
        name="unpack",
    )(rows_grad, small_grad)
    return (
        out, grad, gains, shifts, proj.reshape(OWN, 3, 384), triple_b, dense.T, inner, units.reshape(24), outer.T,
        final.reshape(6),
    )


def solution(mesh):
    placed = (
        P(("dp", "tensor"), None),
        P("dp"),
        P(None, "dp"),
        P(None, "dp"),
        P("dp", None, "tensor"),
        P(None, ("tensor", "dp")),
        P("tensor", "dp"),
        P("dp", "tensor"),
        P(("tensor", "dp")),
        P("tensor", "dp"),
        P("dp"),
        P(("dp", "tensor"), None),
    )
    return jax.shard_map(
        local,
        mesh=mesh,
        in_specs=placed,
        out_specs=(
            P(("dp", "tensor"), None),
            P(("dp", "tensor"), None),
            P(None, ("dp", "tensor")),
            P(None, ("dp", "tensor")),
            P("dp", None, "tensor"),
            P(None, ("tensor", "dp")),
            P("tensor", "dp"),
            P("dp", "tensor"),
            P(("tensor", "dp")),
            P("tensor", "dp"),
            P(("dp", "tensor")),
        ),
        check_vma=False,
    )
```

```python
import math

import jax
import jax.numpy as jnp
import numpy as np
from jax import lax
from jax.experimental import pallas as pl
from jax.experimental.pallas import tpu as pltpu
from jax.sharding import PartitionSpec as P

MESH = pl.DeviceIdType.MESH
F32, BF16 = jnp.float32, jnp.bfloat16

D, HD, ROT = 768, 64, 16
T, HALF_T = 512, 256
EPSILON = 1e-05
Y, XH, Z, CORE = 4, 2, 4, 2
OWN = 12
PAD = 16
BLK = OWN * XH * CORE
COLS, WIDE = 4864, 2432
W_SMALL, W_DENSE, W_UNITS = 1152, 1280, (1792, 3328)
G_COLS, G_WIDE = 4608, 2304
G_DENSE, G_INNER, G_OUTER = 1152, (1536, 3072), (2304, 3840)
EVEN = ((0, 384), (384, 384))
UNEVEN = ((0, 512), (512, 384))
W_GROUPS = ((0, 896, UNEVEN, 0), (1792, 768, EVEN, 896), (3328, 768, EVEN, 1664))
G_GROUPS = ((0, 768, EVEN, 0), (1536, 768, EVEN, 768), (3072, 768, EVEN, 1536))
VEC = 5 * D + 3 * 384 + 1536
OFF_TB, OFF_UB = 5 * OWN, 5 * OWN + 18
VMEM_LIMIT = 56 * 1024 * 1024


def order_tables():
    j = np.arange(64)
    c, xh, z, y = j % 2, (j // 2) % 2, (j // 4) % 4, j // 16
    dp = ((y * 2 + xh) * 4 + z) * 2 + c
    at = (12 * dp[:, None] + np.arange(12)[None, :]).reshape(-1)
    perm = np.zeros((D, D), np.float32)
    perm[at, np.arange(D)] = 1
    spread = np.zeros((128, VEC), np.float32)
    mask = np.zeros((64, VEC), np.float32)
    col = np.arange(D)
    for v in range(5):
        spread[v * 12 + col % 12, v * D + col] = 1
        mask[col // 12, v * D + col] = 1
    back = np.argsort(dp)
    col = np.arange(384)
    for k in range(3):
        spread[OFF_TB + 6 * k + col % 6, 5 * D + 384 * k + col] = 1
        mask[back[col // 6], 5 * D + 384 * k + col] = 1
    col = np.arange(1536)
    spread[OFF_UB + col % 24, 5 * D + 1152 + col] = 1
    mask[back[col // 24], 5 * D + 1152 + col] = 1
    rows = np.zeros((D, 64), np.float32)
    rows[12 * j, j] = 1
    eights = np.zeros((128, 64), np.float32)
    eights[8 * (j // 4) + j % 4, j] = 1
    pick = np.zeros((BLK, 64), np.float32)
    r = np.arange(BLK)
    pick[r, 16 * (r // 12) + r % 12] = 1
    return [m.astype(jnp.bfloat16) for m in (perm, spread, mask, eights, np.ascontiguousarray(rows.T), pick, np.ascontiguousarray(pick.T))]


def nn(a, b):
    return lax.dot_general(a, b, (((1,), (0,)), ((), ())), preferred_element_type=F32)


def nt(a, b):
    return lax.dot_general(a, b, (((1,), (1,)), ((), ())), preferred_element_type=F32)


def tn(a, b):
    return lax.dot_general(a, b, (((0,), (0,)), ((), ())), preferred_element_type=F32)


class Place:
    def __init__(self):
        dp = lax.axis_index("dp")
        self.t = lax.axis_index("tensor")
        self.c = lax.rem(dp, 2)
        self.z = lax.rem(lax.div(dp, 2), 4)
        self.xh = lax.rem(lax.div(dp, 8), 2)
        self.y = lax.div(dp, 16)
        self.slot = self.xh * 2 + self.c

    def dev(self, y=None, xh=None, z=None, c=None, t=None):
        y = self.y if y is None else y
        xh = self.xh if xh is None else xh
        z = self.z if z is None else z
        c = self.c if c is None else c
        t = self.t if t is None else t
        return (((y * 2 + xh) * 4 + z) * 2 + c, t)

    def ring(self, axis, step):
        at = lax.rem((self.y if axis == "y" else self.z) + step, 4)
        return self.dev(y=at) if axis == "y" else self.dev(z=at)

    def quad(self, r):
        c = 1 - self.c if r & 1 else self.c
        xh = 1 - self.xh if r & 2 else self.xh
        return self.dev(xh=xh, c=c), xh, c

    def other(self, r):
        c = 1 - self.c if r & 1 else self.c
        xh = 1 - self.xh if r & 2 else self.xh
        return self.dev(xh=xh, c=c, t=1 - self.t)

    def peers(self):
        out = [self.quad(r)[0] for r in (1, 2, 3)]
        for axis in ("y", "z"):
            out += [self.ring(axis, step) for step in (1, 2, 3)]
        return out + [self.other(r) for r in range(4)]


def enter(place, beside):
    barrier = pltpu.get_barrier_semaphore()
    peers = place.peers()
    for peer in peers:
        pl.semaphore_signal(barrier, inc=1, device_id=peer, device_id_type=MESH)
    beside()
    pl.semaphore_wait(barrier, len(peers))


class Copy:
    def __init__(self, parts):
        self.parts = parts
        self.make().start()

    def make(self):
        src, dst, send, recv, device = self.parts()
        return pltpu.make_async_remote_copy(
            src_ref=src, dst_ref=dst, send_sem=send, recv_sem=recv, device_id=device, device_id_type=MESH
        )

    def wait_recv(self):
        self.make().wait_recv()

    def wait_send(self):
        self.make().wait_send()


def span(begin, width):
    return pl.ds(begin if isinstance(begin, int) else pl.multiple_of(begin, 128), width)


def cut(part, width):
    first = 256 if part == 0 or width == 512 else 128
    return ((0, first), (first, width - first))


class Gather:
    axes = (("y", "z"), ("z", "y"))

    def __init__(self, me, w, sems):
        self.me, self.w = me, w
        self.p0s, self.p0r, self.p1s, self.p1r, self.ss, self.sr = sems
        self.sibling = me.dev(c=1 - me.c)
        self.first, self.second, self.shared = {}, {}, {}

    def cols(self, group, part, piece=None):
        base, half, parts, _ = W_GROUPS[group]
        begin, width = parts[part]
        if piece is not None:
            more, width = cut(part, width)[piece]
            begin += more
        return span(self.me.c * half + (base + begin), width)

    def unit(self, group, part, step, piece=None):
        cols = self.cols(group, part, piece)
        if self.axes[part][1] == "y":
            return self.w.at[lax.rem(self.me.y + step, 4), :, :, cols]
        return self.w.at[:, lax.rem(self.me.z + step, 4), :, cols]

    def share(self, group, part, step):
        def parts():
            ref = self.unit(group, part, step)
            return ref, ref, self.ss.at[group, part, step], self.sr.at[group, part, step], self.sibling

        self.shared[group, part, step] = Copy(parts)

    def start(self, group):
        me = self.me
        for part in range(2):
            for step in (2, 1, 3):

                def parts(part=part, step=step):
                    at = (group, part, step - 1)
                    ref = self.w.at[me.y, me.z, :, self.cols(group, part)]
                    return ref, ref, self.p0s.at[at], self.p0r.at[at], me.ring(self.axes[part][0], step)

                self.first[group, part, step - 1] = Copy(parts)

    def onward(self, group, part, origin, piece, sem, step):
        def parts():
            ref, at = self.unit(group, part, origin, piece), (group, part, sem)
            return ref, ref, self.p1s.at[at], self.p1r.at[at], self.me.ring(self.axes[part][1], step)

        self.second[group, part, sem] = Copy(parts)

    def turn(self, group):
        for part in range(2):
            for step in (1, 3, 2):
                self.first[group, part, step - 1].wait_recv()
            for i, step in enumerate((1, 3)):
                self.onward(group, part, 0, i, i, step)
            for i, step in enumerate((1, 3)):
                self.onward(group, part, 0, 1 - i, 4 + i, step)
            self.share(group, part, 0)

    def forward(self, group):
        for part in range(2):
            for i, step in enumerate((1, 3)):
                self.second[group, part, i].wait_recv()
                self.onward(group, part, 4 - step, i, 2 + i, step)

    def finish(self, group):
        for part in range(2):
            for i, step in enumerate((1, 3)):
                self.second[group, part, 4 + i].wait_recv()
                self.share(group, part, 4 - step)
        for part in range(2):
            for i in range(2):
                self.second[group, part, 2 + i].wait_recv()
            self.share(group, part, 2)

    def done(self, group):
        for part in range(2):
            for step in range(4):
                self.shared[group, part, step].wait_recv()

    def sent(self):
        for copies in (self.first, self.second, self.shared):
            for copy in copies.values():
                copy.wait_send()


class Reduce:
    axes = (("z", "y"), ("y", "z"))

    def __init__(self, me, g, land, ring1, ring2, red, sems):
        self.me, self.g, self.land, self.ring1, self.ring2, self.red = me, g, land, ring1, ring2, red
        self.cs, self.cr, self.p0s, self.p0r, self.p1s, self.p1r = sems
        self.sibling = me.dev(c=1 - me.c)
        self.pulled, self.first, self.second, self.delivered = {}, {}, {}, {}

    def place(self, group, part, piece=None):
        _, _, parts, at = G_GROUPS[group]
        begin, width = parts[part]
        if piece is not None:
            more, width = cut(part, width)[piece]
            begin += more
        return begin, at + begin, width

    def unit(self, group, part, step, piece=None, core=None):
        base, half, _, _ = G_GROUPS[group]
        begin, _, width = self.place(group, part, piece)
        cols = span((self.me.c if core is None else core) * half + (base + begin), width)
        return self.of(self.g, part, step, cols)

    def of(self, ref, part, step, cols):
        if self.axes[part][0] == "y":
            return ref.at[lax.rem(self.me.y + step, 4), :, :, cols]
        return ref.at[:, lax.rem(self.me.z + step, 4), :, cols]

    def landed(self, group, part, step):
        _, at, width = self.place(group, part)
        return self.of(self.land, part, step, span(at, width))

    def add(self, dst, *terms):
        def body(i, carry):
            total = dst[i].astype(F32)
            for term in terms:
                total += term[i].astype(F32)
            dst[i] = total.astype(BF16)
            return carry

        lax.fori_loop(0, 4, body, 0)

    def pull(self, group, part):
        for step in (2, 1, 3, 0):

            def parts(step=step):
                at = (group, part, step)
                src = self.unit(group, part, step, core=1 - self.me.c)
                return src, self.landed(group, part, step), self.cs.at[at], self.cr.at[at], self.sibling

            self.pulled[group, part, step] = Copy(parts)

    def join(self, group, part, step):
        self.pulled[group, part, step].wait_recv()
        self.add(self.unit(group, part, step), self.landed(group, part, step))

    def piece1(self, group, part, i):
        _, at, width = self.place(group, part, i)
        return self.ring1.at[:, :, span(at, width)]

    def start(self, group):
        for part in range(2):
            self.join(group, part, 2)
            for i, step in enumerate((1, 3)):

                def parts(part=part, i=i, step=step):
                    at = (group, part, i)
                    src, dst = self.unit(group, part, 2, i), self.piece1(group, part, i)
                    return src, dst, self.p0s.at[at], self.p0r.at[at], self.me.ring(self.axes[part][0], step)

                self.first[group, part, i] = Copy(parts)
        for part in range(2):
            for i, step in enumerate((1, 3)):
                self.join(group, part, step)
                self.owner(group, part, i, 1 - i, 4 + i, step)

    def owner(self, group, part, i, piece, sem, step):
        def parts():
            at = (group, part, sem)
            src, dst = self.unit(group, part, step, piece), self.whole2(group, part, i, piece)
            return src, dst, self.p0s.at[at], self.p0r.at[at], self.me.ring(self.axes[part][0], step)

        self.first[group, part, sem] = Copy(parts)

    def whole2(self, group, part, i, piece=None):
        _, at, width = self.place(group, part, piece)
        return self.ring2.at[i, :, :, span(at, width)]

    def turn(self, group):
        for part in range(2):
            for i, step in enumerate((1, 3)):
                self.first[group, part, i].wait_recv()
                self.add(self.unit(group, part, step, i), self.piece1(group, part, i))
                self.owner(group, part, i, i, 2 + i, step)

    def across(self, group, part, step):
        me = self.me
        base, half, _, _ = G_GROUPS[group]
        begin, _, width = self.place(group, part)
        cols = span(me.c * half + (base + begin), width)
        if self.axes[part][1] == "y":
            return self.g.at[lax.rem(me.y + step, 4), me.z, :, cols]
        return self.g.at[me.y, lax.rem(me.z + step, 4), :, cols]

    def finish(self, group):
        for part in range(2):
            self.join(group, part, 0)
            for i in range(2):
                self.first[group, part, 4 + i].wait_recv()
                self.first[group, part, 2 + i].wait_recv()
            self.add(self.unit(group, part, 0), self.whole2(group, part, 0), self.whole2(group, part, 1))
            for step in (2, 1, 3):

                def parts(part=part, step=step):
                    _, at, width = self.place(group, part)
                    sem = (group, part, step - 1)
                    src, dst = self.across(group, part, step), self.red.at[step - 1, :, span(at, width)]
                    return src, dst, self.p1s.at[sem], self.p1r.at[sem], self.me.ring(self.axes[part][1], step)

                self.second[group, part, step - 1] = Copy(parts)

    def done(self, group, pick_t, quad):
        for part in range(2):
            _, at, width = self.place(group, part)
            total = self.across(group, part, 0)[...].astype(F32)
            for step in (1, 3, 2):
                self.second[group, part, step - 1].wait_recv()
                total += self.red[step - 1, :, at : at + width].astype(F32)
            quad[:, :, at : at + width] = nn(pick_t[...], total.astype(BF16)).astype(BF16).reshape(4, PAD, width)

    def deliver(self, group, quad, landing, qs, qr):
        me = self.me
        _, half, _, at = G_GROUPS[group]
        for r in (1, 2, 3):

            def parts(r=r):
                device, xh, c = me.quad(r)
                src, dst = quad.at[xh * 2 + c, :, span(at, half)], landing.at[me.slot, :, span(at, half)]
                return src, dst, qs.at[1, group, r], qr.at[1, group, r], device

            self.delivered[group, r] = Copy(parts)
        landing[me.slot, :, at : at + half] = quad[me.slot, :, at : at + half]

    def sent(self):
        for copies in (self.pulled, self.first, self.second, self.delivered):
            for copy in copies.values():
                copy.wait_send()


class Small:
    def __init__(self, me, mine, land_z, land_y, land_q, sends, recvs):
        self.me, self.mine, self.land_z, self.land_y, self.land_q = me, mine, land_z, land_y, land_q
        self.sends, self.recvs, self.copies = sends, recvs, {}

    def copy(self, n, src, dst, device):
        self.copies[n] = Copy(lambda: (src(), dst(), self.sends.at[n], self.recvs.at[n], device()))

    def start(self):
        me = self.me
        for step in (2, 1, 3):
            self.copy(
                step - 1,
                lambda step=step: self.mine.at[:, lax.rem(me.z + step, 4)],
                lambda step=step: self.land_z.at[step - 1],
                lambda step=step: me.ring("z", step),
            )

    def turn(self):
        me = self.me
        for n in range(3):
            self.copies[n].wait_recv()
        self.land_z[3] = self.mine[:, me.z] + self.land_z[0] + self.land_z[1] + self.land_z[2]
        for step in (2, 1, 3):
            self.copy(
                2 + step,
                lambda step=step: self.land_z.at[3, lax.rem(me.y + step, 4)],
                lambda step=step: self.land_y.at[step - 1],
                lambda step=step: me.ring("y", step),
            )

    def finish(self):
        me = self.me
        for n in range(3):
            self.copies[3 + n].wait_recv()
        self.land_y[3] = self.land_z[3, me.y] + self.land_y[0] + self.land_y[1] + self.land_y[2]
        place = me.t * 4 + me.slot
        self.land_q[place] = self.land_y[3]
        for r in range(7):
            self.copy(
                6 + r,
                lambda: self.land_y.at[3],
                lambda: self.land_q.at[me.t * 4 + me.slot],
                lambda r=r: me.quad(r + 1)[0] if r < 3 else me.other(r - 3),
            )

    def done(self):
        me = self.me
        for r in range(7):
            self.copies[6 + r].wait_recv()
        lane = lax.broadcasted_iota(jnp.int32, (8, 128), 1)
        row = lax.broadcasted_iota(jnp.int32, (8, 128), 0)
        total = jnp.zeros((8, 128), F32)
        for n in range(4):
            total += self.land_q[me.t * 4 + n] + jnp.where(lane < 4 * OWN, self.land_q[(1 - me.t) * 4 + n], 0.0)
        return jnp.broadcast_to(jnp.sum(jnp.where(row == me.slot, total, 0.0), axis=0, keepdims=True), (8, 128))

    def sent(self):
        for copy in self.copies.values():
            copy.wait_send()


def rotated(field, cosine, left, right, sign):
    n = field.shape[1]
    return field * cosine + sign * (pltpu.roll(field, n - 8, 1) * left + pltpu.roll(field, 8, 1) * right)


def one_hot(shape, test):
    row = lax.broadcasted_iota(jnp.int32, shape, 0)
    col = lax.broadcasted_iota(jnp.int32, shape, 1)
    return jnp.where(test(row, col), 1.0, 0.0)


def pack(triple, dense, inner, outer, small, mine, rows):
    mine[...] = jnp.zeros_like(mine)
    tall = one_hot((PAD, OWN), lambda r, c: r == c).astype(BF16)
    line = jnp.zeros((1, 128), F32)
    begin = 0
    for ref in small:
        count, width = ref.shape
        for i in range(count):
            put = one_hot((width, 128), lambda r, c, begin=begin: c == r + begin).astype(BF16)
            line += nn(ref[i : i + 1, :], put)
            begin += width
    first = lax.broadcasted_iota(jnp.int32, (PAD, 128), 0) == 0
    rows[...] = jnp.zeros_like(rows)
    for r in range(OWN):
        line3 = triple[r].astype(F32)
        for n in range(3):
            rows[r : r + 1, 384 * n : 384 * n + 384] = line3[n : n + 1, :]
    mine[0, :, 0:896] = rows[:, 0:896].astype(BF16)
    mine[0, :, 896:WIDE] = nn(tall, inner[...]).astype(BF16)
    mine[1, :, 0:256] = rows[:, 896:1152].astype(BF16)
    mine[1, :, 256:384] = jnp.where(first, line, 0.0).astype(BF16)
    mine[1, :, 384:768] = nn(tall, dense[...]).astype(BF16)
    mine[1, :, 896:WIDE] = nn(tall, outer[...]).astype(BF16)


def turn_tables(starts, cos_t, left_t, right_t, bias):
    begin = jnp.broadcast_to(starts[...].astype(F32), (8, T))
    places = lax.broadcasted_iota(jnp.int32, (8, T), 1).astype(F32) - begin
    freqs = jnp.exp(lax.broadcasted_iota(jnp.int32, (8, T), 0).astype(F32) * (-2.0 * math.log(10000.0) / ROT))
    turns = places * freqs

    def spread_lanes(rows, test):
        put = one_hot((8, 128), lambda r, c: (c % 8 == r) & test(c % HD))
        return lax.dot_general(
            rows.T, put, (((1,), (0,)), ((), ())), preferred_element_type=F32, precision=lax.Precision.HIGHEST
        )

    lane = lax.broadcasted_iota(jnp.int32, (1, 128), 1) % HD
    sine = jnp.sin(turns)
    cos_t[...] = spread_lanes(jnp.cos(turns), lambda c: c < ROT) + jnp.where(lane < ROT, 0.0, 1.0)
    left_t[...] = -spread_lanes(sine, lambda c: c < ROT // 2)
    right_t[...] = spread_lanes(sine, lambda c: (c >= ROT // 2) & (c < ROT))
    begin_col = begin.T[:, 0:1]

    def body(i, carry):
        rows = pl.ds(pl.multiple_of(i * 128, 128), 128)
        place_t = i * 128 + lax.broadcasted_iota(jnp.int32, (128, T), 0)
        place_s = lax.broadcasted_iota(jnp.int32, (128, T), 1)
        col = bias[rows, 0:1]
        bias[rows, :] = jnp.where((col == begin[0:1, :]) & (place_s <= place_t), 0.0, -1e30)
        return carry

    bias[:, 0:128] = jnp.broadcast_to(begin_col, (T, 128))
    lax.fori_loop(0, 4, body, 0)


def unpack_kernel(
    rows, small, out_in, grad_in, gains, shifts, triple_b, units, final, proj, dense, inner, outer, out, grad
):
    out[...] = out_in[...]
    grad[...] = grad_in[...]
    side = lax.axis_index("tensor")
    line = jnp.broadcast_to(small[0:1, :], (8, 128))

    def lanes(begin, width):
        put = one_hot((128, width), lambda r, c: r == c + begin)
        picked = lax.dot_general(
            line, put, (((1,), (0,)), ((), ())), preferred_element_type=F32, precision=lax.Precision.HIGHEST
        )
        return picked[0:1, :]

    for i in range(2):
        gains[i : i + 1, :] = lanes(OWN * i + side * 6, 6)
        shifts[i : i + 1, :] = lanes(2 * OWN + OWN * i + side * 6, 6)
    for i in range(3):
        triple_b[i : i + 1, :] = lanes(OFF_TB + 6 * i, 6)
    units[...] = lanes(OFF_UB, 24)
    final[...] = lanes(4 * OWN + side * 6, 6)
    for n in range(3):
        proj[:, n, :] = rows[0, 0:OWN, 384 * n : 384 * n + 384] if n < 2 else rows[1, 0:OWN, 0:384]
    inner[...] = rows[0, 0:OWN, 768:2304]
    dense[...] = rows[1, 0:OWN, 384:768]
    outer[...] = rows[1, 0:OWN, 768:2304]


def kernel(
    triple, dense, inner_w, outer_w, gains, shifts, fbias, tbias, ubias, starts, x, cot,
    perm, spread, mask, rows_at, rows_of, pick, pick_t,
    out, grad, small_out, rows_out,
    w, g, land, ring1, ring2, red, quad_in, quad_out, quad_land, x_land, cot_land, out_send, out_land, nb_send, nb_land,
    small_mine, small_z, small_y, small_q,
    s1, s2, up, s1t, s2t, upt, hat, fac, q, k, v, cb, ctx, tb, act, ub, outp, nbp, vec, gvec,
    mine, cos_t, left_t, right_t, bias, slope, rows_in,
    ap0s, ap0r, ap1s, ap1r, ass, asr, rcs, rcr, rp0s, rp0r, rp1s, rp1r, qs, qr, ts, tr, es, er,
):
    me = Place()
    enter(me, lambda: pack(triple, dense, inner_w, outer_w, (gains, shifts, fbias, tbias, ubias), mine, rows_in))
    partner = me.dev(t=1 - me.t)
    gather = Gather(me, w, (ap0s, ap0r, ap1s, ap1r, ass, asr))
    reduce = Reduce(me, g, land, ring1, ring2, red, (rcs, rcr, rp0s, rp0r, rp1s, rp1r))
    minor = Small(me, small_mine, small_z, small_y, small_q, es, er)
    quads, swaps = {}, []
    for group, (_, half, _, at) in enumerate(W_GROUPS):
        for r in (1, 2, 3):

            def parts(group=group, half=half, at=at, r=r):
                device, _, c = me.quad(r)
                src, dst = mine.at[c, :, span(at, half)], quad_in.at[me.slot, :, span(at, half)]
                return src, dst, qs.at[0, group, r], qr.at[0, group, r], device

            quads[group, r] = Copy(parts)

    def swap(i, src, dst):
        swaps.append(Copy(lambda: (src, dst, ts.at[i], tr.at[i], partner)))

    quad_in[me.slot] = mine[me.c]
    gvec[...] = jnp.zeros_like(gvec)
    turn_tables(starts, cos_t, left_t, right_t, bias)
    swap(0, x, x_land)

    def block(group):
        base, half, _, at = W_GROUPS[group]
        for r in (1, 2, 3):
            quads[group, r].wait_recv()
        rows = quad_in[:, :, at : at + half].reshape(64, half)
        w[me.y, me.z, :, span(me.c * half + base, half)] = nn(pick[...], rows).astype(BF16)
        gather.start(group)

    block(0)
    swap(1, cot, cot_land)
    def norm_rows(x_ref, first_row):
        rows = pl.ds(pl.multiple_of(first_row, HALF_T), HALF_T)
        hat[rows, :] = nn(x_ref[...], perm[...])

        def body(i, carry):
            at = pl.ds(pl.multiple_of(first_row + i * 64, 64), 64)
            field = hat[at, :]
            centred = field - jnp.mean(field, axis=-1, keepdims=True)
            factor = lax.rsqrt(jnp.mean(centred * centred, axis=-1, keepdims=True) + EPSILON)
            hat[at, :] = centred * factor
            fac[at, :] = jnp.broadcast_to(factor, (64, 128))
            return carry

        lax.fori_loop(0, 4, body, 0)

    def back_rows(cot_ref, first_row):
        rows = pl.ds(pl.multiple_of(first_row, HALF_T), HALF_T)
        up[rows, :] = nn(cot_ref[...], perm[...]).astype(BF16)

        def body(i, carry):
            at = pl.ds(pl.multiple_of(first_row + i * 128, 128), 128)
            upstream = up[at, :]
            upt[:, at] = upstream.T
            gvec[0:1, 4 * D : 5 * D] += jnp.sum(upstream.astype(F32), axis=0, keepdims=True)
            return carry

        lax.fori_loop(0, 2, body, 0)

    norm_rows(x, me.t * HALF_T)
    gather.turn(0)
    back_rows(cot, me.t * HALF_T)
    gather.forward(0)
    block(1)
    swaps[0].wait_recv()
    norm_rows(x_land, (1 - me.t) * HALF_T)
    gather.finish(0)
    gather.turn(1)
    block(2)
    gather.done(0)

    def wcols(begin, width):
        return w[:, :, :, span(begin, width)].reshape(D, width)

    def wrows(i, begin, width):
        return w[2 * i : 2 * i + 2, :, :, begin : begin + width].reshape(384, width)

    def put(i, begin, value):
        width = value.shape[1]
        g[2 * i : 2 * i + 2, :, :, begin : begin + width] = value.astype(BF16).reshape(2, Z, BLK, width)

    small = nn(rows_of[...], wcols(W_SMALL, 128)).astype(BF16)
    for begin in range(0, VEC, D):
        width = min(D, VEC - begin)
        cols = slice(begin, begin + width)
        picked = nn(small, spread[:, cols]) * mask[:, cols].astype(F32)
        vec[:, cols] = jnp.broadcast_to(jnp.sum(picked, axis=0, keepdims=True), (8, width))

    def rowvec(begin, width):
        return vec[0:1, span(begin, width)]

    g0, g1, h0, h1, fb = (vec[0:1, i * D : (i + 1) * D] for i in range(5))

    def scale_rows(i, carry):
        rows = pl.ds(pl.multiple_of(i * 128, 128), 128)
        normal = hat[rows, :]
        first = (normal * g0 + h0).astype(BF16)
        second = (normal * g1 + h1).astype(BF16)
        s1[rows, :] = first
        s2[rows, :] = second
        s1t[:, rows] = first.T
        s2t[:, rows] = second.T
        return carry

    lax.fori_loop(0, 4, scale_rows, 0)

    scale = 1.0 / math.sqrt(HD)

    def thrice(table):
        return jnp.concatenate([table[...]] * 3, axis=1)

    for n, ref in enumerate((q, k, v)):
        field = nn(s1[...], wcols(n * 384, 384)) + rowvec(5 * D + n * 384, 384)
        if n < 2:
            field = rotated(field, thrice(cos_t), thrice(left_t), thrice(right_t), 1.0)
        field = field.astype(BF16)
        ref[...] = field * BF16(scale) if n == 0 else field
    swaps[1].wait_recv()
    back_rows(cot_land, (1 - me.t) * HALF_T)
    cb[...] = nn(up[...], wcols(W_DENSE, 384)).astype(BF16)
    gather.forward(1)

    def attend(pair, carry):
        cols = span(pair * 128, 128)
        halves = []
        for head in range(2):
            inside = (lax.broadcasted_iota(jnp.int32, (1, 128), 1) // HD) == head
            grads_k, grads_v, outs, grads_q = [], [], [], []
            for block in range(2):
                begin, n = block * HALF_T, (block + 1) * HALF_T
                rows = slice(begin, begin + HALF_T)
                kk, vv = k[0:n, cols], v[0:n, cols]
                qq = jnp.where(inside, q[rows, cols], 0).astype(BF16)
                cc = jnp.where(inside, cb[rows, cols], 0).astype(BF16)
                scores = nt(qq, kk) + bias[rows, 0:n]
                powers = jnp.exp(scores - jnp.max(scores, axis=-1, keepdims=True))
                probs = powers * (1.0 / jnp.sum(powers, axis=-1, keepdims=True))
                low = probs.astype(BF16)
                outs.append(nn(low, vv))
                back = nt(cc, vv)
                inner = jnp.sum(probs * back, axis=-1, keepdims=True)
                ds = (probs * (back - inner)).astype(BF16)
                grads_q.append(nn(ds, kk) * scale)
                grads_k.append(tn(ds, qq))
                grads_v.append(tn(low, cc))
            join = lambda parts: jnp.concatenate([parts[1][:HALF_T] + parts[0], parts[1][HALF_T:]], axis=0)
            halves.append(
                (jnp.concatenate(outs, axis=0), jnp.concatenate(grads_q, axis=0), join(grads_k), join(grads_v))
            )
        first = (lax.broadcasted_iota(jnp.int32, (1, 128), 1) // HD) == 0
        result, dq, dk, dv = (jnp.where(first, a, b) for a, b in zip(*halves))
        ctx[:, cols] = result.astype(BF16)
        for n, field in enumerate((dq, dk, dv)):
            if n < 2:
                field = rotated(field, cos_t[...], left_t[...], right_t[...], -1.0)
            field = field.astype(BF16)
            tb[:, span(n * 384 + pair * 128, 128)] = field
            gvec[0:1, span(5 * D + n * 384 + pair * 128, 128)] = jnp.sum(field.astype(F32), axis=0, keepdims=True)

        @pl.when(pair == 0)
        def _():
            gather.finish(1)
            gather.turn(2)

        @pl.when(pair == 1)
        def _():
            gather.forward(2)

        return carry

    lax.fori_loop(0, 3, attend, 0)
    gather.finish(2)

    for i in range(2):
        rows = slice(384 * i, 384 * i + 384)
        put(i, 0, nn(s1t[rows, :], tb[...]))
        put(i, G_DENSE, nn(upt[rows, :], ctx[...]))
    for part in range(2):
        reduce.pull(0, part)
    for i in range(2):
        rows = slice(384 * i, 384 * i + 384)
        outp[:, rows] = nt(ctx[...], wrows(i, W_DENSE, 384))
    gather.done(1)

    own = me.t * HALF_T
    other = pl.ds(pl.multiple_of((1 - me.t) * HALF_T, HALF_T), HALF_T)

    def units(half):
        def body(i, carry):
            cols = span(half * 768 + i * 256, 256)
            lane = 5 * D + 1152 + half * 768 + i * 256
            pre = nn(s2[...], wcols(W_UNITS[half] + i * 256, 256)) + rowvec(lane, 256)
            phi = 0.5 * (1.0 + lax.erf(pre * (1.0 / math.sqrt(2.0))))
            act[:, cols] = (pre * phi).astype(BF16)
            slope[:, cols] = phi + pre * jnp.exp(-0.5 * pre * pre) * (1.0 / math.sqrt(2.0 * math.pi))
            return carry

        lax.fori_loop(0, 3, body, 0)

    def units_back(half):
        def body(i, carry):
            cols = span(half * 768 + i * 256, 256)
            back = (nn(up[...], wcols(W_UNITS[half] + 768 + i * 256, 256)) * slope[:, cols]).astype(BF16)
            ub[:, cols] = back
            lane = 5 * D + 1152 + half * 768 + i * 256
            gvec[0:1, span(lane, 256)] = jnp.sum(back.astype(F32), axis=0, keepdims=True)
            return carry

        lax.fori_loop(0, 3, body, 0)

    def grads(half):
        cols = slice(768 * half, 768 * half + 768)
        for i in range(2):
            rows = slice(384 * i, 384 * i + 384)
            put(i, G_INNER[half], nn(s2t[rows, :], ub[:, cols]))
            put(i, G_OUTER[half], nn(upt[rows, :], act[:, cols]))
        for part in range(2):
            reduce.pull(1 + half, part)

    units(0)
    reduce.start(0)
    gather.done(2)
    units(1)
    for i in range(2):
        rows = slice(384 * i, 384 * i + 384)
        outp[:, rows] += nt(act[:, 0:768], wrows(i, W_UNITS[0] + 768, 768))
        outp[:, rows] += nt(act[:, 768:1536], wrows(i, W_UNITS[1] + 768, 768))
    out_send[...] = outp[other, :].astype(BF16)
    swap(2, out_send, out_land)
    units_back(0)
    reduce.turn(0)
    grads(0)
    units_back(1)
    reduce.finish(0)
    reduce.start(1)
    grads(1)
    for i in range(2):
        rows = slice(384 * i, 384 * i + 384)
        first = nt(tb[...], wrows(i, 0, 1152))
        second = nt(ub[:, 0:768], wrows(i, W_UNITS[0], 768)) + nt(ub[:, 768:1536], wrows(i, W_UNITS[1], 768))
        nbp[:, rows] = first * vec[0:1, rows] + second * vec[0:1, D + 384 * i : D + 384 * i + 384]
        normal = hat[:, rows]
        for n, term in enumerate((first * normal, second * normal, first, second)):
            gvec[0:1, n * D + 384 * i : n * D + 384 * i + 384] = jnp.sum(term, axis=0, keepdims=True)
    nb_send[...] = nbp[other, :].astype(BF16)
    swap(3, nb_send, nb_land)
    reduce.start(2)
    reduce.done(0, pick_t, quad_out)
    reduce.deliver(0, quad_out, quad_land, qs, qr)
    reduce.turn(1)
    tile = jnp.zeros((64, 128), F32)
    for begin in range(0, VEC, D):
        width = min(D, VEC - begin)
        cols = slice(begin, begin + width)
        tile += nt((gvec[0:1, cols] * mask[:, cols].astype(F32)).astype(BF16), spread[:, cols])
    small_mine[...] = nn(rows_at[...], tile.astype(BF16)).reshape(Y, Z, 8, 128)
    minor.start()
    reduce.finish(1)
    reduce.turn(2)
    minor.turn()
    reduce.done(1, pick_t, quad_out)
    reduce.deliver(1, quad_out, quad_land, qs, qr)
    minor.finish()
    reduce.finish(2)
    for copy in swaps[2:]:
        copy.wait_recv()

    low = nn(x[...], perm[...]) + outp[pl.ds(pl.multiple_of(own, HALF_T), HALF_T), :] + out_land[...].astype(F32) + fb
    out[...] = nt(low.astype(BF16), perm[...]).astype(BF16)

    def finish_rows(i, carry):
        rows = pl.ds(pl.multiple_of(i * 64, 64), 64)
        mine_at = pl.ds(pl.multiple_of(own + i * 64, 64), 64)
        back = nbp[mine_at, :] + nb_land[rows, :].astype(F32)
        normal = hat[mine_at, :]
        value = up[mine_at, :].astype(F32) + fac[mine_at, 0:1] * (
            back
            - jnp.mean(back, axis=-1, keepdims=True)
            - normal * jnp.mean(back * normal, axis=-1, keepdims=True)
        )
        x_land[rows, :] = value.astype(BF16)
        return carry

    lax.fori_loop(0, 4, finish_rows, 0)
    grad[...] = nt(x_land[...], perm[...]).astype(BF16)
    reduce.done(2, pick_t, quad_out)
    reduce.deliver(2, quad_out, quad_land, qs, qr)
    small_out[...] = minor.done()
    for copy in reduce.delivered.values():
        copy.wait_recv()
    for c in range(2):
        rows_out[c] = quad_land[c].astype(F32) + quad_land[2 + c].astype(F32)
    for copy in list(quads.values()) + swaps:
        copy.wait_send()
    gather.sent()
    reduce.sent()
    minor.sent()


def local(
    layer_input, segment_starts, norm_gains, norm_shifts, projection, triple_bias, dense_weight, inner_weight,
    unit_bias, outer_weight, final_bias, cotangent,
):
    vm = pl.BlockSpec(memory_space=pltpu.VMEM)
    dma = pltpu.SemaphoreType.DMA
    struct = jax.ShapeDtypeStruct
    vmem = pltpu.VMEM
    out, grad, small_grad, rows_grad = pl.pallas_call(
        kernel,
        out_shape=(
            struct((HALF_T, D), BF16), struct((HALF_T, D), BF16), struct((8, 128), F32), struct((2, PAD, G_WIDE), F32),
        ),
        in_specs=[vm] * 19,
        out_specs=(vm,) * 4,
        scratch_shapes=[
            vmem((Y, Z, BLK, COLS), BF16), vmem((Y, Z, BLK, G_COLS), BF16), vmem((Y, Z, BLK, G_WIDE), BF16),
            vmem((4, BLK, G_WIDE), BF16), vmem((2, 4, BLK, G_WIDE), BF16), vmem((3, BLK, G_WIDE), BF16),
            vmem((4, PAD, WIDE), BF16), vmem((4, PAD, G_WIDE), BF16), vmem((4, PAD, G_WIDE), BF16),
        ]
        + [vmem((HALF_T, D), BF16)] * 6
        + [vmem((Y, Z, 8, 128), F32), vmem((4, 4, 8, 128), F32), vmem((4, 8, 128), F32), vmem((8, 8, 128), F32)]
        + [vmem((T, D), BF16)] * 3
        + [vmem((D, T), BF16)] * 3
        + [vmem((T, D), F32), vmem((T, 128), F32)]
        + [vmem((T, 384), BF16)] * 5
        + [vmem((T, 1152), BF16), vmem((T, 1536), BF16), vmem((T, 1536), BF16)]
        + [vmem((T, D), F32)] * 2
        + [vmem((8, VEC), F32)] * 2
        + [vmem((2, PAD, WIDE), BF16)]
        + [vmem((T, 128), F32)] * 3
        + [vmem((T, T), F32), vmem((T, 1536), F32), vmem((PAD, 1152), F32)]
        + [dma((3, 2, 3))] * 2
        + [dma((3, 2, 6))] * 2
        + [dma((3, 2, 4))] * 4
        + [dma((3, 2, 6))] * 2
        + [dma((3, 2, 3))] * 2
        + [dma((2, 3, 4))] * 2
        + [dma((4,))] * 2
        + [dma((13,))] * 2,
        compiler_params=pltpu.CompilerParams(collective_id=0, has_side_effects=True, vmem_limit_bytes=VMEM_LIMIT),
        name="layer",
    )(
        projection, dense_weight.T, inner_weight, outer_weight.T, norm_gains, norm_shifts,
        final_bias.reshape(1, OWN), triple_bias, unit_bias.reshape(1, 24), segment_starts.reshape(1, T),
        layer_input, cotangent, *[jnp.asarray(m) for m in order_tables()],
    )
    gains, shifts, triple_b, units, final, proj, dense, inner, outer, out, grad = pl.pallas_call(
        unpack_kernel,
        out_shape=(
            struct((2, 6), F32), struct((2, 6), F32), struct((3, 6), F32), struct((1, 24), F32), struct((1, 6), F32),
            struct((OWN, 3, 384), F32), struct((OWN, 384), F32), struct((OWN, 1536), F32), struct((OWN, 1536), F32),
            struct((HALF_T, D), BF16), struct((HALF_T, D), BF16),
        ),
        in_specs=[vm] * 4,
        out_specs=(vm,) * 11,
        name="unpack",
    )(rows_grad, small_grad, out, grad)
    return (
        out, grad, gains, shifts, proj, triple_b, dense.T, inner, units.reshape(24), outer.T,
        final.reshape(6),
    )


def solution(mesh):
    placed = (
        P(("dp", "tensor"), None),
        P("dp"),
        P(None, "dp"),
        P(None, "dp"),
        P("dp", None, "tensor"),
        P(None, ("tensor", "dp")),
        P("tensor", "dp"),
        P("dp", "tensor"),
        P(("tensor", "dp")),
        P("tensor", "dp"),
        P("dp"),
        P(("dp", "tensor"), None),
    )
    return jax.shard_map(
        local,
        mesh=mesh,
        in_specs=placed,
        out_specs=(
            P(("dp", "tensor"), None),
            P(("dp", "tensor"), None),
            P(None, ("dp", "tensor")),
            P(None, ("dp", "tensor")),
            P("dp", None, "tensor"),
            P(None, ("tensor", "dp")),
            P("tensor", "dp"),
            P("dp", "tensor"),
            P(("tensor", "dp")),
            P("tensor", "dp"),
            P(("dp", "tensor")),
        ),
        check_vma=False,
    )
```

```python
import math

import jax
import jax.numpy as jnp
import numpy as np
from jax import lax
from jax.experimental import pallas as pl
from jax.experimental.pallas import tpu as pltpu
from jax.sharding import PartitionSpec as P

MESH = pl.DeviceIdType.MESH
F32, BF16 = jnp.float32, jnp.bfloat16

D, HD, ROT = 768, 64, 16
T, HALF_T = 512, 256
EPSILON = 1e-05
Y, XH, Z, CORE = 4, 2, 4, 2
OWN = 12
PAD = 16
BLK = OWN * XH * CORE
COLS, WIDE = 4864, 2432
W_SMALL, W_DENSE, W_UNITS = 1152, 1280, (1792, 3328)
G_COLS, G_WIDE = 4608, 2304
G_DENSE, G_INNER, G_OUTER = 1152, (1536, 3072), (2304, 3840)
EVEN = ((0, 384), (384, 384))
UNEVEN = ((0, 512), (512, 384))
W_GROUPS = ((0, 896, UNEVEN, 0), (1792, 768, EVEN, 896), (3328, 768, EVEN, 1664))
G_GROUPS = ((0, 768, EVEN, 0), (1536, 768, EVEN, 768), (3072, 768, EVEN, 1536))
VEC = 5 * D + 3 * 384 + 1536
OFF_TB, OFF_UB = 5 * OWN, 5 * OWN + 18
VMEM_LIMIT = 56 * 1024 * 1024


def order_tables():
    j = np.arange(64)
    c, xh, z, y = j % 2, (j // 2) % 2, (j // 4) % 4, j // 16
    dp = ((y * 2 + xh) * 4 + z) * 2 + c
    at = (12 * dp[:, None] + np.arange(12)[None, :]).reshape(-1)
    perm = np.zeros((D, D), np.float32)
    perm[at, np.arange(D)] = 1
    spread = np.zeros((128, VEC), np.float32)
    mask = np.zeros((64, VEC), np.float32)
    col = np.arange(D)
    for v in range(5):
        spread[v * 12 + col % 12, v * D + col] = 1
        mask[col // 12, v * D + col] = 1
    back = np.argsort(dp)
    col = np.arange(384)
    for k in range(3):
        spread[OFF_TB + 6 * k + col % 6, 5 * D + 384 * k + col] = 1
        mask[back[col // 6], 5 * D + 384 * k + col] = 1
    col = np.arange(1536)
    spread[OFF_UB + col % 24, 5 * D + 1152 + col] = 1
    mask[back[col // 24], 5 * D + 1152 + col] = 1
    rows = np.zeros((D, 64), np.float32)
    rows[12 * j, j] = 1
    eights = np.zeros((128, 64), np.float32)
    eights[8 * (j // 4) + j % 4, j] = 1
    pick = np.zeros((BLK, 64), np.float32)
    r = np.arange(BLK)
    pick[r, 16 * (r // 12) + r % 12] = 1
    return [m.astype(jnp.bfloat16) for m in (perm, spread, mask, eights, np.ascontiguousarray(rows.T), pick, np.ascontiguousarray(pick.T))]


def nn(a, b):
    return lax.dot_general(a, b, (((1,), (0,)), ((), ())), preferred_element_type=F32)


def nt(a, b):
    return lax.dot_general(a, b, (((1,), (1,)), ((), ())), preferred_element_type=F32)


def tn(a, b):
    return lax.dot_general(a, b, (((0,), (0,)), ((), ())), preferred_element_type=F32)


class Place:
    def __init__(self):
        dp = lax.axis_index("dp")
        self.t = lax.axis_index("tensor")
        self.c = lax.rem(dp, 2)
        self.z = lax.rem(lax.div(dp, 2), 4)
        self.xh = lax.rem(lax.div(dp, 8), 2)
        self.y = lax.div(dp, 16)
        self.slot = self.xh * 2 + self.c

    def dev(self, y=None, xh=None, z=None, c=None, t=None):
        y = self.y if y is None else y
        xh = self.xh if xh is None else xh
        z = self.z if z is None else z
        c = self.c if c is None else c
        t = self.t if t is None else t
        return (((y * 2 + xh) * 4 + z) * 2 + c, t)

    def ring(self, axis, step):
        at = lax.rem((self.y if axis == "y" else self.z) + step, 4)
        return self.dev(y=at) if axis == "y" else self.dev(z=at)

    def quad(self, r):
        c = 1 - self.c if r & 1 else self.c
        xh = 1 - self.xh if r & 2 else self.xh
        return self.dev(xh=xh, c=c), xh, c

    def other(self, r):
        c = 1 - self.c if r & 1 else self.c
        xh = 1 - self.xh if r & 2 else self.xh
        return self.dev(xh=xh, c=c, t=1 - self.t)

    def peers(self):
        out = [self.quad(r)[0] for r in (1, 2, 3)]
        for axis in ("y", "z"):
            out += [self.ring(axis, step) for step in (1, 2, 3)]
        return out + [self.other(r) for r in range(4)]


def enter(place, beside):
    barrier = pltpu.get_barrier_semaphore()
    peers = place.peers()
    for peer in peers:
        pl.semaphore_signal(barrier, inc=1, device_id=peer, device_id_type=MESH)
    beside()
    pl.semaphore_wait(barrier, len(peers))


class Copy:
    def __init__(self, parts):
        self.parts = parts
        self.make().start()

    def make(self):
        src, dst, send, recv, device = self.parts()
        return pltpu.make_async_remote_copy(
            src_ref=src, dst_ref=dst, send_sem=send, recv_sem=recv, device_id=device, device_id_type=MESH
        )

    def wait_recv(self):
        self.make().wait_recv()

    def wait_send(self):
        self.make().wait_send()


def span(begin, width):
    return pl.ds(begin if isinstance(begin, int) else pl.multiple_of(begin, 128), width)


def cut(part, width):
    first = 256 if part == 0 or width == 512 else 128
    return ((0, first), (first, width - first))


class Gather:
    axes = (("y", "z"), ("z", "y"))

    def __init__(self, me, w, sems):
        self.me, self.w = me, w
        self.p0s, self.p0r, self.p1s, self.p1r, self.ss, self.sr = sems
        self.sibling = me.dev(c=1 - me.c)
        self.first, self.second, self.shared = {}, {}, {}

    def cols(self, group, part, piece=None):
        base, half, parts, _ = W_GROUPS[group]
        begin, width = parts[part]
        if piece is not None:
            more, width = cut(part, width)[piece]
            begin += more
        return span(self.me.c * half + (base + begin), width)

    def unit(self, group, part, step, piece=None):
        cols = self.cols(group, part, piece)
        if self.axes[part][1] == "y":
            return self.w.at[lax.rem(self.me.y + step, 4), :, :, cols]
        return self.w.at[:, lax.rem(self.me.z + step, 4), :, cols]

    def share(self, group, part, step):
        def parts():
            ref = self.unit(group, part, step)
            return ref, ref, self.ss.at[group, part, step], self.sr.at[group, part, step], self.sibling

        self.shared[group, part, step] = Copy(parts)

    def start(self, group):
        me = self.me
        for part in range(2):
            for step in (2, 1, 3):

                def parts(part=part, step=step):
                    at = (group, part, step - 1)
                    ref = self.w.at[me.y, me.z, :, self.cols(group, part)]
                    return ref, ref, self.p0s.at[at], self.p0r.at[at], me.ring(self.axes[part][0], step)

                self.first[group, part, step - 1] = Copy(parts)

    def onward(self, group, part, origin, piece, sem, step):
        def parts():
            ref, at = self.unit(group, part, origin, piece), (group, part, sem)
            return ref, ref, self.p1s.at[at], self.p1r.at[at], self.me.ring(self.axes[part][1], step)

        self.second[group, part, sem] = Copy(parts)

    def turn(self, group):
        for part in range(2):
            for step in (1, 3, 2):
                self.first[group, part, step - 1].wait_recv()
            for i, step in enumerate((1, 3)):
                self.onward(group, part, 0, i, i, step)
            for i, step in enumerate((1, 3)):
                self.onward(group, part, 0, 1 - i, 4 + i, step)
            if group == 0:
                self.share(group, part, 0)

    def forward(self, group):
        for part in range(2):
            for i, step in enumerate((1, 3)):
                self.second[group, part, i].wait_recv()
                self.onward(group, part, 4 - step, i, 2 + i, step)

    def finish(self, group):
        for part in range(2):
            for i, step in enumerate((1, 3)):
                self.second[group, part, 4 + i].wait_recv()
                if group == 0:
                    self.share(group, part, 4 - step)
        for part in range(2):
            for i in range(2):
                self.second[group, part, 2 + i].wait_recv()
            if group == 0:
                self.share(group, part, 2)
        if group > 0:

            def parts():
                base, half, _, _ = W_GROUPS[group]
                ref = self.w.at[:, :, :, span(self.me.c * half + base, half)]
                return ref, ref, self.ss.at[group, 0, 0], self.sr.at[group, 0, 0], self.sibling

            self.shared[group, 0, 0] = Copy(parts)

    def done(self, group):
        for at, copy in self.shared.items():
            if at[0] == group:
                copy.wait_recv()

    def sent(self):
        for copies in (self.first, self.second, self.shared):
            for copy in copies.values():
                copy.wait_send()


class Reduce:
    axes = (("z", "y"), ("y", "z"))

    def __init__(self, me, g, land, ring1, ring2, red, sems):
        self.me, self.g, self.land, self.ring1, self.ring2, self.red = me, g, land, ring1, ring2, red
        self.cs, self.cr, self.p0s, self.p0r, self.p1s, self.p1r = sems
        self.sibling = me.dev(c=1 - me.c)
        self.pulled, self.first, self.second, self.delivered = {}, {}, {}, {}

    def place(self, group, part, piece=None):
        _, _, parts, at = G_GROUPS[group]
        begin, width = parts[part]
        if piece is not None:
            more, width = cut(part, width)[piece]
            begin += more
        return begin, at + begin, width

    def unit(self, group, part, step, piece=None, core=None):
        base, half, _, _ = G_GROUPS[group]
        begin, _, width = self.place(group, part, piece)
        cols = span((self.me.c if core is None else core) * half + (base + begin), width)
        return self.of(self.g, part, step, cols)

    def of(self, ref, part, step, cols):
        if self.axes[part][0] == "y":
            return ref.at[lax.rem(self.me.y + step, 4), :, :, cols]
        return ref.at[:, lax.rem(self.me.z + step, 4), :, cols]

    def add(self, dst, *terms):
        def body(i, carry):
            if len(terms) == 1:
                dst[i] = dst[i] + terms[0][i]
                return carry
            total = dst[i].astype(F32)
            for term in terms:
                total += term[i].astype(F32)
            dst[i] = total.astype(BF16)
            return carry

        lax.fori_loop(0, 4, body, 0)

    def pull(self, group):
        base, half, _, at = G_GROUPS[group]

        def parts():
            src = self.g.at[:, :, :, span((1 - self.me.c) * half + base, half)]
            dst = self.land.at[:, :, :, span(at, half)]
            return src, dst, self.cs.at[group], self.cr.at[group], self.sibling

        self.pulled[group] = Copy(parts)

    def join(self, group):
        self.pulled[group].wait_recv()
        base, half, _, at = G_GROUPS[group]
        cols = span(self.me.c * half + base, half)

        def body(i, carry):
            y, z = lax.div(i, 4), lax.rem(i, 4)
            self.g[y, z, :, cols] = self.g[y, z, :, cols] + self.land[y, z, :, at : at + half]
            return carry

        lax.fori_loop(0, 16, body, 0)

    def piece1(self, group, part, i):
        _, at, width = self.place(group, part, i)
        return self.ring1.at[:, :, span(at, width)]

    def start(self, group):
        self.join(group)
        for part in range(2):
            for i, step in enumerate((1, 3)):

                def parts(part=part, i=i, step=step):
                    at = (group, part, i)
                    src, dst = self.unit(group, part, 2, i), self.piece1(group, part, i)
                    return src, dst, self.p0s.at[at], self.p0r.at[at], self.me.ring(self.axes[part][0], step)

                self.first[group, part, i] = Copy(parts)
        for part in range(2):
            for i, step in enumerate((1, 3)):
                self.owner(group, part, i, 1 - i, 4 + i, step)

    def owner(self, group, part, i, piece, sem, step):
        def parts():
            at = (group, part, sem)
            src, dst = self.unit(group, part, step, piece), self.whole2(group, part, i, piece)
            return src, dst, self.p0s.at[at], self.p0r.at[at], self.me.ring(self.axes[part][0], step)

        self.first[group, part, sem] = Copy(parts)

    def whole2(self, group, part, i, piece=None):
        _, at, width = self.place(group, part, piece)
        return self.ring2.at[i, :, :, span(at, width)]

    def turn(self, group):
        for part in range(2):
            for i, step in enumerate((1, 3)):
                self.first[group, part, i].wait_recv()
                self.add(self.unit(group, part, step, i), self.piece1(group, part, i))
                self.owner(group, part, i, i, 2 + i, step)

    def across(self, group, part, step):
        me = self.me
        base, half, _, _ = G_GROUPS[group]
        begin, _, width = self.place(group, part)
        cols = span(me.c * half + (base + begin), width)
        if self.axes[part][1] == "y":
            return self.g.at[lax.rem(me.y + step, 4), me.z, :, cols]
        return self.g.at[me.y, lax.rem(me.z + step, 4), :, cols]

    def finish(self, group):
        for part in range(2):
            for i in range(2):
                self.first[group, part, 4 + i].wait_recv()
                self.first[group, part, 2 + i].wait_recv()
            self.add(self.unit(group, part, 0), self.whole2(group, part, 0), self.whole2(group, part, 1))
            for step in (2, 1, 3):

                def parts(part=part, step=step):
                    _, at, width = self.place(group, part)
                    sem = (group, part, step - 1)
                    src, dst = self.across(group, part, step), self.red.at[step - 1, :, span(at, width)]
                    return src, dst, self.p1s.at[sem], self.p1r.at[sem], self.me.ring(self.axes[part][1], step)

                self.second[group, part, step - 1] = Copy(parts)

    def done(self, group, pick_t, quad):
        for part in range(2):
            _, at, width = self.place(group, part)
            total = self.across(group, part, 0)[...].astype(F32)
            for step in (1, 3, 2):
                self.second[group, part, step - 1].wait_recv()
                total += self.red[step - 1, :, at : at + width].astype(F32)
            quad[:, :, at : at + width] = nn(pick_t[...], total.astype(BF16)).astype(BF16).reshape(4, PAD, width)

    def deliver(self, group, quad, landing, qs, qr):
        me = self.me
        _, half, _, at = G_GROUPS[group]
        for r in (1, 2, 3):

            def parts(r=r):
                device, xh, c = me.quad(r)
                src, dst = quad.at[xh * 2 + c, :, span(at, half)], landing.at[me.slot, :, span(at, half)]
                return src, dst, qs.at[1, group, r], qr.at[1, group, r], device

            self.delivered[group, r] = Copy(parts)
        landing[me.slot, :, at : at + half] = quad[me.slot, :, at : at + half]

    def sent(self):
        for copies in (self.pulled, self.first, self.second, self.delivered):
            for copy in copies.values():
                copy.wait_send()


class Small:
    def __init__(self, me, mine, land_z, land_y, land_q, sends, recvs):
        self.me, self.mine, self.land_z, self.land_y, self.land_q = me, mine, land_z, land_y, land_q
        self.sends, self.recvs, self.copies = sends, recvs, {}

    def copy(self, n, src, dst, device):
        self.copies[n] = Copy(lambda: (src(), dst(), self.sends.at[n], self.recvs.at[n], device()))

    def start(self):
        me = self.me
        for step in (2, 1, 3):
            self.copy(
                step - 1,
                lambda step=step: self.mine.at[:, lax.rem(me.z + step, 4)],
                lambda step=step: self.land_z.at[step - 1],
                lambda step=step: me.ring("z", step),
            )

    def turn(self):
        me = self.me
        for n in range(3):
            self.copies[n].wait_recv()
        self.land_z[3] = self.mine[:, me.z] + self.land_z[0] + self.land_z[1] + self.land_z[2]
        for step in (2, 1, 3):
            self.copy(
                2 + step,
                lambda step=step: self.land_z.at[3, lax.rem(me.y + step, 4)],
                lambda step=step: self.land_y.at[step - 1],
                lambda step=step: me.ring("y", step),
            )

    def finish(self):
        me = self.me
        for n in range(3):
            self.copies[3 + n].wait_recv()
        self.land_y[3] = self.land_z[3, me.y] + self.land_y[0] + self.land_y[1] + self.land_y[2]
        place = me.t * 4 + me.slot
        self.land_q[place] = self.land_y[3]
        for r in range(7):
            self.copy(
                6 + r,
                lambda: self.land_y.at[3],
                lambda: self.land_q.at[me.t * 4 + me.slot],
                lambda r=r: me.quad(r + 1)[0] if r < 3 else me.other(r - 3),
            )

    def done(self):
        me = self.me
        for r in range(7):
            self.copies[6 + r].wait_recv()
        lane = lax.broadcasted_iota(jnp.int32, (8, 128), 1)
        row = lax.broadcasted_iota(jnp.int32, (8, 128), 0)
        total = jnp.zeros((8, 128), F32)
        for n in range(4):
            total += self.land_q[me.t * 4 + n] + jnp.where(lane < 4 * OWN, self.land_q[(1 - me.t) * 4 + n], 0.0)
        return jnp.broadcast_to(jnp.sum(jnp.where(row == me.slot, total, 0.0), axis=0, keepdims=True), (8, 128))

    def sent(self):
        for copy in self.copies.values():
            copy.wait_send()


def rotated(field, cosine, left, right, sign):
    n = field.shape[1]
    return field * cosine + sign * (pltpu.roll(field, n - 8, 1) * left + pltpu.roll(field, 8, 1) * right)


def one_hot(shape, test):
    row = lax.broadcasted_iota(jnp.int32, shape, 0)
    col = lax.broadcasted_iota(jnp.int32, shape, 1)
    return jnp.where(test(row, col), 1.0, 0.0)


def pack(triple, dense, inner, outer, small, mine, rows):
    mine[...] = jnp.zeros_like(mine)
    tall = one_hot((PAD, OWN), lambda r, c: r == c).astype(BF16)
    line = jnp.zeros((1, 128), F32)
    begin = 0
    for ref in small:
        count, width = ref.shape
        for i in range(count):
            put = one_hot((width, 128), lambda r, c, begin=begin: c == r + begin).astype(BF16)
            line += nn(ref[i : i + 1, :], put)
            begin += width
    first = lax.broadcasted_iota(jnp.int32, (PAD, 128), 0) == 0
    rows[...] = jnp.zeros_like(rows)
    for r in range(OWN):
        line3 = triple[r].astype(F32)
        for n in range(3):
            rows[r : r + 1, 384 * n : 384 * n + 384] = line3[n : n + 1, :]
    mine[0, :, 0:896] = rows[:, 0:896].astype(BF16)
    mine[0, :, 896:WIDE] = nn(tall, inner[...]).astype(BF16)
    mine[1, :, 0:256] = rows[:, 896:1152].astype(BF16)
    mine[1, :, 256:384] = jnp.where(first, line, 0.0).astype(BF16)
    mine[1, :, 384:768] = nn(tall, dense[...]).astype(BF16)
    mine[1, :, 896:WIDE] = nn(tall, outer[...]).astype(BF16)


def turn_tables(starts, cos_t, left_t, right_t, bias):
    begin = jnp.broadcast_to(starts[...].astype(F32), (8, T))
    places = lax.broadcasted_iota(jnp.int32, (8, T), 1).astype(F32) - begin
    freqs = jnp.exp(lax.broadcasted_iota(jnp.int32, (8, T), 0).astype(F32) * (-2.0 * math.log(10000.0) / ROT))
    turns = places * freqs

    def spread_lanes(rows, test):
        put = one_hot((8, 128), lambda r, c: (c % 8 == r) & test(c % HD))
        return lax.dot_general(
            rows.T, put, (((1,), (0,)), ((), ())), preferred_element_type=F32, precision=lax.Precision.HIGHEST
        )

    lane = lax.broadcasted_iota(jnp.int32, (1, 128), 1) % HD
    sine = jnp.sin(turns)
    cos_t[...] = spread_lanes(jnp.cos(turns), lambda c: c < ROT) + jnp.where(lane < ROT, 0.0, 1.0)
    left_t[...] = -spread_lanes(sine, lambda c: c < ROT // 2)
    right_t[...] = spread_lanes(sine, lambda c: (c >= ROT // 2) & (c < ROT))
    begin_col = begin.T[:, 0:1]

    def body(i, carry):
        rows = pl.ds(pl.multiple_of(i * 128, 128), 128)
        place_t = i * 128 + lax.broadcasted_iota(jnp.int32, (128, T), 0)
        place_s = lax.broadcasted_iota(jnp.int32, (128, T), 1)
        col = bias[rows, 0:1]
        bias[rows, :] = jnp.where((col == begin[0:1, :]) & (place_s <= place_t), 0.0, -1e30)
        return carry

    bias[:, 0:128] = jnp.broadcast_to(begin_col, (T, 128))
    lax.fori_loop(0, 4, body, 0)


def unpack_kernel(
    rows, small, out_in, grad_in, gains, shifts, triple_b, units, final, proj, dense, inner, outer, out, grad
):
    out[...] = out_in[...]
    grad[...] = grad_in[...]
    side = lax.axis_index("tensor")
    line = jnp.broadcast_to(small[0:1, :], (8, 128))

    def product(rows_in, put):
        return lax.dot_general(
            rows_in, put, (((1,), (0,)), ((), ())), preferred_element_type=F32, precision=lax.Precision.HIGHEST
        )

    row = lax.broadcasted_iota(jnp.int32, (8, 128), 0)
    lane = lax.broadcasted_iota(jnp.int32, (8, 128), 1)
    begin = jnp.where(row < 5, 2 * row + side, row + 5) * 6
    held = jnp.where((lane >= begin) & (lane < begin + 6), line, 0.0)
    sixes = product(held, one_hot((128, 6), lambda r, c: r % 6 == c))
    gains[...] = sixes[0:2, :]
    shifts[...] = sixes[2:4, :]
    final[...] = sixes[4:5, :]
    triple_b[...] = sixes[5:8, :]
    units[...] = product(line, one_hot((128, 24), lambda r, c: r == c + OFF_UB))[0:1, :]
    for n in range(3):
        proj[:, n, :] = rows[0, 0:OWN, 384 * n : 384 * n + 384] if n < 2 else rows[1, 0:OWN, 0:384]
    inner[...] = rows[0, 0:OWN, 768:2304]
    dense[...] = rows[1, 0:OWN, 384:768]
    outer[...] = rows[1, 0:OWN, 768:2304]


def kernel(
    triple, dense, inner_w, outer_w, gains, shifts, fbias, tbias, ubias, starts, x, cot,
    perm, spread, mask, rows_at, rows_of, pick, pick_t,
    out, grad, small_out, rows_out,
    w, g, land, ring1, ring2, red, quad_in, quad_out, quad_land, x_land, cot_land, out_send, out_land, nb_send, nb_land,
    small_mine, small_z, small_y, small_q,
    s1, s2, up, s1t, s2t, upt, hat, fac, q, k, v, cb, ctx, tb, act, ub, outp, nbp, vec, gvec,
    mine, cos_t, left_t, right_t, bias, slope, rows_in,
    ap0s, ap0r, ap1s, ap1r, ass, asr, rcs, rcr, rp0s, rp0r, rp1s, rp1r, qs, qr, ts, tr, es, er,
):
    me = Place()
    enter(me, lambda: pack(triple, dense, inner_w, outer_w, (gains, shifts, fbias, tbias, ubias), mine, rows_in))
    partner = me.dev(t=1 - me.t)
    gather = Gather(me, w, (ap0s, ap0r, ap1s, ap1r, ass, asr))
    reduce = Reduce(me, g, land, ring1, ring2, red, (rcs, rcr, rp0s, rp0r, rp1s, rp1r))
    minor = Small(me, small_mine, small_z, small_y, small_q, es, er)
    quads, swaps = {}, []
    for group, (_, half, _, at) in enumerate(W_GROUPS):
        for r in (1, 2, 3):

            def parts(group=group, half=half, at=at, r=r):
                device, _, c = me.quad(r)
                src, dst = mine.at[c, :, span(at, half)], quad_in.at[me.slot, :, span(at, half)]
                return src, dst, qs.at[0, group, r], qr.at[0, group, r], device

            quads[group, r] = Copy(parts)

    def swap(i, src, dst):
        swaps.append(Copy(lambda: (src, dst, ts.at[i], tr.at[i], partner)))

    quad_in[me.slot] = mine[me.c]
    gvec[...] = jnp.zeros_like(gvec)
    turn_tables(starts, cos_t, left_t, right_t, bias)
    swap(0, x, x_land)

    def block(group):
        base, half, _, at = W_GROUPS[group]
        for r in (1, 2, 3):
            quads[group, r].wait_recv()
        rows = quad_in[:, :, at : at + half].reshape(64, half)
        w[me.y, me.z, :, span(me.c * half + base, half)] = nn(pick[...], rows).astype(BF16)
        gather.start(group)

    block(0)
    swap(1, cot, cot_land)
    def norm_rows(x_ref, first_row):
        rows = pl.ds(pl.multiple_of(first_row, HALF_T), HALF_T)
        hat[rows, :] = nn(x_ref[...], perm[...])

        def body(i, carry):
            at = pl.ds(pl.multiple_of(first_row + i * 64, 64), 64)
            field = hat[at, :]
            centred = field - jnp.mean(field, axis=-1, keepdims=True)
            factor = lax.rsqrt(jnp.mean(centred * centred, axis=-1, keepdims=True) + EPSILON)
            hat[at, :] = centred * factor
            fac[at, :] = jnp.broadcast_to(factor, (64, 128))
            return carry

        lax.fori_loop(0, 4, body, 0)

    def back_rows(cot_ref, first_row):
        rows = pl.ds(pl.multiple_of(first_row, HALF_T), HALF_T)
        up[rows, :] = nn(cot_ref[...], perm[...]).astype(BF16)

        def body(i, carry):
            at = pl.ds(pl.multiple_of(first_row + i * 128, 128), 128)
            upstream = up[at, :]
            upt[:, at] = upstream.T
            gvec[0:1, 4 * D : 5 * D] += jnp.sum(upstream.astype(F32), axis=0, keepdims=True)
            return carry

        lax.fori_loop(0, 2, body, 0)

    norm_rows(x, me.t * HALF_T)
    gather.turn(0)
    back_rows(cot, me.t * HALF_T)
    gather.forward(0)
    block(1)
    swaps[0].wait_recv()
    norm_rows(x_land, (1 - me.t) * HALF_T)
    gather.finish(0)
    gather.turn(1)
    block(2)
    gather.done(0)

    def wcols(begin, width):
        return w[:, :, :, span(begin, width)].reshape(D, width)

    def wrows(i, begin, width):
        return w[2 * i : 2 * i + 2, :, :, begin : begin + width].reshape(384, width)

    def put(i, begin, value):
        width = value.shape[1]
        g[2 * i : 2 * i + 2, :, :, begin : begin + width] = value.astype(BF16).reshape(2, Z, BLK, width)

    small = nn(rows_of[...], wcols(W_SMALL, 128)).astype(BF16)
    for begin in range(0, VEC, D):
        width = min(D, VEC - begin)
        cols = slice(begin, begin + width)
        picked = nn(small, spread[:, cols]) * mask[:, cols].astype(F32)
        vec[:, cols] = jnp.broadcast_to(jnp.sum(picked, axis=0, keepdims=True), (8, width))

    def rowvec(begin, width):
        return vec[0:1, span(begin, width)]

    g0, g1, h0, h1, fb = (vec[0:1, i * D : (i + 1) * D] for i in range(5))

    def scale_rows(i, carry):
        rows = pl.ds(pl.multiple_of(i * 128, 128), 128)
        normal = hat[rows, :]
        first = (normal * g0 + h0).astype(BF16)
        second = (normal * g1 + h1).astype(BF16)
        s1[rows, :] = first
        s2[rows, :] = second
        s1t[:, rows] = first.T
        s2t[:, rows] = second.T
        return carry

    lax.fori_loop(0, 4, scale_rows, 0)

    scale = 1.0 / math.sqrt(HD)

    def thrice(table):
        return jnp.concatenate([table[...]] * 3, axis=1)

    for n, ref in enumerate((q, k, v)):
        field = nn(s1[...], wcols(n * 384, 384)) + rowvec(5 * D + n * 384, 384)
        if n < 2:
            field = rotated(field, thrice(cos_t), thrice(left_t), thrice(right_t), 1.0)
        field = field.astype(BF16)
        ref[...] = field * BF16(scale) if n == 0 else field
    swaps[1].wait_recv()
    back_rows(cot_land, (1 - me.t) * HALF_T)
    cb[...] = nn(up[...], wcols(W_DENSE, 384)).astype(BF16)
    gather.forward(1)

    def attend(pair, carry):
        cols = span(pair * 128, 128)
        halves = []
        for head in range(2):
            inside = (lax.broadcasted_iota(jnp.int32, (1, 128), 1) // HD) == head
            grads_k, grads_v, outs, grads_q = [], [], [], []
            for block in range(2):
                begin, n = block * HALF_T, (block + 1) * HALF_T
                rows = slice(begin, begin + HALF_T)
                kk, vv = k[0:n, cols], v[0:n, cols]
                qq = jnp.where(inside, q[rows, cols], 0).astype(BF16)
                cc = jnp.where(inside, cb[rows, cols], 0).astype(BF16)
                scores = nt(qq, kk) + bias[rows, 0:n]
                powers = jnp.exp(scores - jnp.max(scores, axis=-1, keepdims=True))
                probs = powers * (1.0 / jnp.sum(powers, axis=-1, keepdims=True))
                low = probs.astype(BF16)
                outs.append(nn(low, vv))
                back = nt(cc, vv)
                inner = jnp.sum(probs * back, axis=-1, keepdims=True)
                ds = (probs * (back - inner)).astype(BF16)
                grads_q.append(nn(ds, kk) * scale)
                grads_k.append(tn(ds, qq))
                grads_v.append(tn(low, cc))
            join = lambda parts: jnp.concatenate([parts[1][:HALF_T] + parts[0], parts[1][HALF_T:]], axis=0)
            halves.append(
                (jnp.concatenate(outs, axis=0), jnp.concatenate(grads_q, axis=0), join(grads_k), join(grads_v))
            )
        first = (lax.broadcasted_iota(jnp.int32, (1, 128), 1) // HD) == 0
        result, dq, dk, dv = (jnp.where(first, a, b) for a, b in zip(*halves))
        ctx[:, cols] = result.astype(BF16)
        for n, field in enumerate((dq, dk, dv)):
            if n < 2:
                field = rotated(field, cos_t[...], left_t[...], right_t[...], -1.0)
            field = field.astype(BF16)
            tb[:, span(n * 384 + pair * 128, 128)] = field
            gvec[0:1, span(5 * D + n * 384 + pair * 128, 128)] = jnp.sum(field.astype(F32), axis=0, keepdims=True)

        @pl.when(pair == 0)
        def _():
            gather.finish(1)
            gather.turn(2)

        @pl.when(pair == 1)
        def _():
            gather.forward(2)

        return carry

    lax.fori_loop(0, 3, attend, 0)
    gather.finish(2)

    for i in range(2):
        rows = slice(384 * i, 384 * i + 384)
        put(i, 0, nn(s1t[rows, :], tb[...]))
        put(i, G_DENSE, nn(upt[rows, :], ctx[...]))
    reduce.pull(0)
    for i in range(2):
        rows = slice(384 * i, 384 * i + 384)
        outp[:, rows] = nt(ctx[...], wrows(i, W_DENSE, 384))
    gather.done(1)

    own = me.t * HALF_T
    other = pl.ds(pl.multiple_of((1 - me.t) * HALF_T, HALF_T), HALF_T)

    def units(half):
        def body(i, carry):
            cols = span(half * 768 + i * 256, 256)
            lane = 5 * D + 1152 + half * 768 + i * 256
            pre = nn(s2[...], wcols(W_UNITS[half] + i * 256, 256)) + rowvec(lane, 256)
            phi = 0.5 * (1.0 + lax.erf(pre * (1.0 / math.sqrt(2.0))))
            act[:, cols] = (pre * phi).astype(BF16)
            slope[:, cols] = phi + pre * jnp.exp(-0.5 * pre * pre) * (1.0 / math.sqrt(2.0 * math.pi))
            return carry

        lax.fori_loop(0, 3, body, 0)

    def units_back(half):
        def body(i, carry):
            cols = span(half * 768 + i * 256, 256)
            back = (nn(up[...], wcols(W_UNITS[half] + 768 + i * 256, 256)) * slope[:, cols]).astype(BF16)
            ub[:, cols] = back
            lane = 5 * D + 1152 + half * 768 + i * 256
            gvec[0:1, span(lane, 256)] = jnp.sum(back.astype(F32), axis=0, keepdims=True)
            return carry

        lax.fori_loop(0, 3, body, 0)

    def grads(half):
        cols = slice(768 * half, 768 * half + 768)
        for i in range(2):
            rows = slice(384 * i, 384 * i + 384)
            put(i, G_INNER[half], nn(s2t[rows, :], ub[:, cols]))
            put(i, G_OUTER[half], nn(upt[rows, :], act[:, cols]))
        reduce.pull(1 + half)

    units(0)
    reduce.start(0)
    units_back(0)
    grads(0)
    reduce.turn(0)
    gather.done(2)
    units(1)
    reduce.start(1)
    for i in range(2):
        rows = slice(384 * i, 384 * i + 384)
        outp[:, rows] += nt(act[:, 0:768], wrows(i, W_UNITS[0] + 768, 768))
        outp[:, rows] += nt(act[:, 768:1536], wrows(i, W_UNITS[1] + 768, 768))
    out_send[...] = outp[other, :].astype(BF16)
    swap(2, out_send, out_land)
    units_back(1)
    reduce.finish(0)
    grads(1)
    for i in range(2):
        rows = slice(384 * i, 384 * i + 384)
        first = nt(tb[...], wrows(i, 0, 1152))
        second = nt(ub[:, 0:768], wrows(i, W_UNITS[0], 768)) + nt(ub[:, 768:1536], wrows(i, W_UNITS[1], 768))
        nbp[:, rows] = first * vec[0:1, rows] + second * vec[0:1, D + 384 * i : D + 384 * i + 384]
        normal = hat[:, rows]
        for n, term in enumerate((first * normal, second * normal, first, second)):
            gvec[0:1, n * D + 384 * i : n * D + 384 * i + 384] = jnp.sum(term, axis=0, keepdims=True)
    nb_send[...] = nbp[other, :].astype(BF16)
    swap(3, nb_send, nb_land)
    reduce.turn(1)
    reduce.start(2)
    reduce.done(0, pick_t, quad_out)
    reduce.deliver(0, quad_out, quad_land, qs, qr)
    tile = jnp.zeros((64, 128), F32)
    for begin in range(0, VEC, D):
        width = min(D, VEC - begin)
        cols = slice(begin, begin + width)
        tile += nt((gvec[0:1, cols] * mask[:, cols].astype(F32)).astype(BF16), spread[:, cols])
    small_mine[...] = nn(rows_at[...], tile.astype(BF16)).reshape(Y, Z, 8, 128)
    minor.start()
    reduce.finish(1)
    reduce.turn(2)
    minor.turn()
    reduce.done(1, pick_t, quad_out)
    reduce.deliver(1, quad_out, quad_land, qs, qr)
    minor.finish()
    reduce.finish(2)
    for copy in swaps[2:]:
        copy.wait_recv()

    low = nn(x[...], perm[...]) + outp[pl.ds(pl.multiple_of(own, HALF_T), HALF_T), :] + out_land[...].astype(F32) + fb
    out[...] = nt(low.astype(BF16), perm[...]).astype(BF16)

    def finish_rows(i, carry):
        rows = pl.ds(pl.multiple_of(i * 64, 64), 64)
        mine_at = pl.ds(pl.multiple_of(own + i * 64, 64), 64)
        back = nbp[mine_at, :] + nb_land[rows, :].astype(F32)
        normal = hat[mine_at, :]
        value = up[mine_at, :].astype(F32) + fac[mine_at, 0:1] * (
            back
            - jnp.mean(back, axis=-1, keepdims=True)
            - normal * jnp.mean(back * normal, axis=-1, keepdims=True)
        )
        x_land[rows, :] = value.astype(BF16)
        return carry

    lax.fori_loop(0, 4, finish_rows, 0)
    grad[...] = nt(x_land[...], perm[...]).astype(BF16)
    reduce.done(2, pick_t, quad_out)
    reduce.deliver(2, quad_out, quad_land, qs, qr)
    small_out[...] = minor.done()
    for copy in reduce.delivered.values():
        copy.wait_recv()
    for c in range(2):
        rows_out[c] = quad_land[c].astype(F32) + quad_land[2 + c].astype(F32)
    for copy in list(quads.values()) + swaps:
        copy.wait_send()
    gather.sent()
    reduce.sent()
    minor.sent()


def local(
    layer_input, segment_starts, norm_gains, norm_shifts, projection, triple_bias, dense_weight, inner_weight,
    unit_bias, outer_weight, final_bias, cotangent,
):
    vm = pl.BlockSpec(memory_space=pltpu.VMEM)
    dma = pltpu.SemaphoreType.DMA
    struct = jax.ShapeDtypeStruct
    vmem = pltpu.VMEM
    out, grad, small_grad, rows_grad = pl.pallas_call(
        kernel,
        out_shape=(
            struct((HALF_T, D), BF16), struct((HALF_T, D), BF16), struct((8, 128), F32), struct((2, PAD, G_WIDE), F32),
        ),
        in_specs=[vm] * 19,
        out_specs=(vm,) * 4,
        scratch_shapes=[
            vmem((Y, Z, BLK, COLS), BF16), vmem((Y, Z, BLK, G_COLS), BF16), vmem((Y, Z, BLK, G_WIDE), BF16),
            vmem((4, BLK, G_WIDE), BF16), vmem((2, 4, BLK, G_WIDE), BF16), vmem((3, BLK, G_WIDE), BF16),
            vmem((4, PAD, WIDE), BF16), vmem((4, PAD, G_WIDE), BF16), vmem((4, PAD, G_WIDE), BF16),
        ]
        + [vmem((HALF_T, D), BF16)] * 6
        + [vmem((Y, Z, 8, 128), F32), vmem((4, 4, 8, 128), F32), vmem((4, 8, 128), F32), vmem((8, 8, 128), F32)]
        + [vmem((T, D), BF16)] * 3
        + [vmem((D, T), BF16)] * 3
        + [vmem((T, D), F32), vmem((T, 128), F32)]
        + [vmem((T, 384), BF16)] * 5
        + [vmem((T, 1152), BF16), vmem((T, 1536), BF16), vmem((T, 1536), BF16)]
        + [vmem((T, D), F32)] * 2
        + [vmem((8, VEC), F32)] * 2
        + [vmem((2, PAD, WIDE), BF16)]
        + [vmem((T, 128), F32)] * 3
        + [vmem((T, T), F32), vmem((T, 1536), F32), vmem((PAD, 1152), F32)]
        + [dma((3, 2, 3))] * 2
        + [dma((3, 2, 6))] * 2
        + [dma((3, 2, 4))] * 2
        + [dma((3,))] * 2
        + [dma((3, 2, 6))] * 2
        + [dma((3, 2, 3))] * 2
        + [dma((2, 3, 4))] * 2
        + [dma((4,))] * 2
        + [dma((13,))] * 2,
        compiler_params=pltpu.CompilerParams(collective_id=0, has_side_effects=True, vmem_limit_bytes=VMEM_LIMIT),
        name="layer",
    )(
        projection, dense_weight.T, inner_weight, outer_weight.T, norm_gains, norm_shifts,
        final_bias.reshape(1, OWN), triple_bias, unit_bias.reshape(1, 24), segment_starts.reshape(1, T),
        layer_input, cotangent, *[jnp.asarray(m) for m in order_tables()],
    )
    gains, shifts, triple_b, units, final, proj, dense, inner, outer, out, grad = pl.pallas_call(
        unpack_kernel,
        out_shape=(
            struct((2, 6), F32), struct((2, 6), F32), struct((3, 6), F32), struct((1, 24), F32), struct((1, 6), F32),
            struct((OWN, 3, 384), F32), struct((OWN, 384), F32), struct((OWN, 1536), F32), struct((OWN, 1536), F32),
            struct((HALF_T, D), BF16), struct((HALF_T, D), BF16),
        ),
        in_specs=[vm] * 4,
        out_specs=(vm,) * 11,
        name="unpack",
    )(rows_grad, small_grad, out, grad)
    return (
        out, grad, gains, shifts, proj, triple_b, dense.T, inner, units.reshape(24), outer.T,
        final.reshape(6),
    )


def solution(mesh):
    placed = (
        P(("dp", "tensor"), None),
        P("dp"),
        P(None, "dp"),
        P(None, "dp"),
        P("dp", None, "tensor"),
        P(None, ("tensor", "dp")),
        P("tensor", "dp"),
        P("dp", "tensor"),
        P(("tensor", "dp")),
        P("tensor", "dp"),
        P("dp"),
        P(("dp", "tensor"), None),
    )
    return jax.shard_map(
        local,
        mesh=mesh,
        in_specs=placed,
        out_specs=(
            P(("dp", "tensor"), None),
            P(("dp", "tensor"), None),
            P(None, ("dp", "tensor")),
            P(None, ("dp", "tensor")),
            P("dp", None, "tensor"),
            P(None, ("tensor", "dp")),
            P("tensor", "dp"),
            P("dp", "tensor"),
            P(("tensor", "dp")),
            P("tensor", "dp"),
            P(("dp", "tensor")),
        ),
        check_vma=False,
    )
```
